128 devices in a mesh: src: 8 (over y, core), tgt: 16 (over x, z).
Axes of the slice: x: 4, y: 4, z: 4, core: 2. Of those that a mesh axis runs over, the one named last changes fastest.
Arguments:
- sources: float32 [256, 16384], P('tgt', 'src'), may hold values from -24 to 24, as said below
- targets: float32 [256, 16384], P('src', 'tgt'), may hold values from -24 to 24, as said below
- source_logw: float32 [16384], P('src'), may hold values from -1 to 1
- target_logw: float32 [16384], P('tgt'), may hold values from -1 to 1
- times: float32 [16384], P('src'), may hold values from 0 to 1
Outputs:
- row_potential: float32 [16384], P('src')
- moved: float32 [256, 16384], P('tgt', 'src')
- col_potential: float32 [16384], P('tgt')
The draws below stay inside these ranges and needn't reach their ends.
Inputs may be any that keep to these rules, and one draw needn't show every extreme that they name: `sources`: point coordinates. `targets`: point coordinates.
All inputs are finite; a program needn't handle non-finite values.
Results may differ from the reference program's by a relative error of at most 0.00025.
Values sent between devices are 32-bit elements; how exact they have to be, the bound alone decides.
A program may use at most 64 MiB of HBM per device.

```python
import math
import jax
import jax.numpy as jnp
import numpy as np
from jax import lax

F = 256
ITERS = 2
NS = 16384
NT = 16384


def paired_points(key):
    keys = jax.random.split(jax.random.fold_in(key, 7), 5)
    clusters = max(NT // 32, 4)
    spread = math.sqrt(32.0 / math.sqrt(2.0 * F))
    centre_scale = math.sqrt(240.0 / F)
    centres = centre_scale * jax.random.normal(keys[0], (clusters, F), jnp.float32)
    target_ids = jax.random.randint(keys[1], (NT,), 0, clusters)
    source_ids = jax.random.randint(keys[2], (NS,), 0, clusters)
    target_pts = centres[target_ids] + spread * jax.random.normal(keys[3], (NT, F), jnp.float32)
    source_pts = centres[source_ids] + spread * jax.random.normal(keys[4], (NS, F), jnp.float32)
    far_rows = np.arange(4) * (NS // 4) + 2
    offset = 68.0 / math.sqrt(F)
    source_pts = source_pts.at[far_rows].add(offset)
    return (jnp.clip(source_pts, -24.0, 24.0), jnp.clip(target_pts, -24.0, 24.0))


def draw_sources(key, part):
    return paired_points(key)[0].T


def draw_targets(key, part):
    return paired_points(key)[1].T


def steps_of(key, extent, pieces, smallest, top_value):
    def one(position, blocks):
        heights = jax.random.uniform(jax.random.fold_in(jax.random.fold_in(key, 6), position), (blocks,), jnp.float32, smallest / len(pieces), top_value / len(pieces))
        return jnp.repeat(jnp.exp(heights), extent[position] // blocks).reshape((-1,) + (1,) * (len(extent) - position - 1))

    level = one(*pieces[0])
    for cut in pieces[1:]:
        level = level * one(*cut)
    return level


def setup_inputs(seed: int = 0) -> dict:
    key_list = jax.random.split(jax.random.key(seed), 6)
    sources = draw_sources(jax.random.fold_in(key_list[5], 71), 0)
    targets = draw_targets(jax.random.fold_in(key_list[5], 71), 0)
    source_logw = jnp.clip(jax.random.uniform(key_list[2], (NS,), jnp.float32, -1.0, 1.0) * steps_of(key_list[2], (NS,), ((0, 8),), -0.4, 0.0), -1.0, 1.0)
    target_logw = jnp.clip(jax.random.uniform(key_list[3], (NT,), jnp.float32, -1.0, 1.0) * steps_of(key_list[3], (NT,), ((0, 16),), -0.4, 0.0), -1.0, 1.0)
    times = jnp.clip(1.0 * jax.random.uniform(key_list[4], (NS,), jnp.float32) ** steps_of(key_list[4], (NS,), ((0, 8),), -0.2, 0.2), 0.0, 1.0)
    return {"sources": sources, "targets": targets, "source_logw": source_logw, "target_logw": target_logw, "times": times}


EPSILON = 16.0


def cost_block(rows, cols):
    cross = jnp.dot(rows, cols.T, precision=lax.Precision.HIGHEST, preferred_element_type=jnp.float32)
    return 0.5 * jnp.sum(rows * rows, 1)[:, None] + 0.5 * jnp.sum(cols * cols, 1)[None, :] - cross


def row_lse(points, targets, col_pot, block):
    count = points.shape[0] // block

    def one(blk):
        scores = (col_pot[None, :] - cost_block(blk, targets)) / EPSILON
        top = jnp.max(scores, 1)
        return top + jnp.log(jnp.sum(jnp.exp(scores - top[:, None]), 1))

    return lax.map(one, points.reshape(count, block, points.shape[1])).reshape(points.shape[0])


def col_lse(points, targets, row_pot, block):
    count = points.shape[0] // block
    cols = targets.shape[0]

    def step(carry, item):
        top, total = carry
        blk, pot = item
        scores = (pot[:, None] - cost_block(blk, targets)) / EPSILON
        fresh = jnp.maximum(top, jnp.max(scores, 0))
        total = total * jnp.exp(top - fresh) + jnp.sum(jnp.exp(scores - fresh[None, :]), 0)
        return (fresh, total), None

    init = (jnp.full((cols,), -1e30, jnp.float32), jnp.zeros((cols,), jnp.float32))
    (top, total), _ = lax.scan(step, init, (points.reshape(count, block, points.shape[1]), row_pot.reshape(count, block)))
    return top + jnp.log(total)


def reference(sources, targets, source_logw, target_logw, times):
    sources = sources.T
    targets = targets.T
    block = min(512, NS)
    col_pot = jnp.zeros((NT,), jnp.float32)
    row_pot = jnp.zeros((NS,), jnp.float32)
    for sweep in range(ITERS):
        row_pot = EPSILON * (source_logw - row_lse(sources, targets, col_pot, block))
        col_pot = EPSILON * (target_logw - col_lse(sources, targets, row_pot, block))
    count = NS // block

    def transport(item):
        blk, pot = item
        plan = jnp.exp((pot[:, None] + col_pot[None, :] - cost_block(blk, targets)) / EPSILON)
        weighted = jnp.dot(plan, targets, precision=lax.Precision.HIGHEST, preferred_element_type=jnp.float32)
        return weighted, jnp.sum(plan, 1)

    weighted, mass = lax.map(transport, (sources.reshape(count, block, F), row_pot.reshape(count, block)))
    weighted = weighted.reshape(NS, F)
    mass = mass.reshape(NS)
    moved = (1.0 - times)[:, None] * sources + times[:, None] * (weighted / mass[:, None])
    final_pot = EPSILON * (target_logw - col_lse(moved, targets, row_pot, block))
    return row_pot, moved.T, final_pot
```

```python
import functools

import jax
import jax.numpy as jnp
from jax import lax
from jax.experimental import pallas as pl
from jax.experimental.pallas import tpu as pltpu
from jax.sharding import PartitionSpec as P

MESH = pl.DeviceIdType.MESH
F32 = jnp.float32
BF16 = jnp.bfloat16
EPSILON = 16.0
LOG2E = 1.4426950408889634
LN2 = 0.6931471805599453
SCALE = LOG2E / EPSILON

FEATURES = 256
ROWS = 2048
COLS = 1024
SIDE = 4
PLANE = 16
LINE = 8
COPIES = 240


def halves(a):
    high = a.astype(BF16)
    return high, (a - high.astype(F32)).astype(BF16)


def kernel(
    src, tgt, slw, tlw, tim,
    rowp, moved, colp,
    sg, tg, mg, tcat, scat, q, e, w, tw, eh, el,
    r1, r2, q1, q2, vr, vc, nb, sb, cb, lrow, frow, phi,
    send_sem, recv_sem,
):
    me_s, me_t = lax.axis_index("src"), lax.axis_index("tgt")
    x, z = me_t // SIDE, me_t % SIDE
    y, core = me_s // 2, me_s % 2
    started = []

    def send(source, target, device):
        k = len(started)
        copy = pltpu.make_async_remote_copy(
            src_ref=source, dst_ref=target, send_sem=send_sem.at[k], recv_sem=recv_sem.at[k],
            device_id=device, device_id_type=MESH,
        )
        copy.start()
        started.append(copy)
        return copy

    def wrap(value):
        return lax.rem(value + SIDE, SIDE)

    def tgt_at(dx, dz):
        return wrap(x + dx) * SIDE + wrap(z + dz)

    def plane_dev(dx, dz):
        return (me_s, tgt_at(dx, dz))

    def at(h, first, second):
        return (first, second) if h == 0 else (second, first)

    barrier = pltpu.get_barrier_semaphore()
    for k in range(1, PLANE):
        pl.semaphore_signal(barrier, inc=1, device_id=(me_s, lax.rem(me_t + k, PLANE)), device_id_type=MESH)
    for k in range(1, LINE):
        pl.semaphore_signal(barrier, inc=1, device_id=(lax.rem(me_s + k, LINE), me_t), device_id_type=MESH)
    pl.semaphore_wait(barrier, PLANE + LINE - 2)

    def slot(buf, h, first, second, cols):
        owner = tgt_at(*at(h, first, second))
        return buf.at[pl.ds(pl.multiple_of(owner * 16 + 8 * h, 8), 8), cols]

    class Gather:
        shifts = (0, -1, 1, 2)

        def __init__(self, own, buf, c0, width):
            self.buf, self.c0, self.width = buf, c0, width
            self.full = pl.ds(c0, width)
            self.parts = (pl.ds(c0, width // 2), pl.ds(c0 + width // 2, width // 2))
            self.c = {}
            for h in (0, 1):
                mine = own.at[pl.ds(8 * h, 8), self.full]
                dst = slot(buf, h, 0, 0, self.full)
                for d in (1, -1):
                    self.c[h, "p1", d] = send(mine, dst, plane_dev(*at(h, d, 0)))
                    self.c[h, 0, d] = send(mine, dst, plane_dev(*at(h, 0, d)))

        def spread(self, h, j):
            ref = slot(self.buf, h, self.shifts[j], 0, self.full)
            for d in (1, -1):
                self.c[h, j, d] = send(ref, ref, plane_dev(*at(h, 0, d)))

        def first_ring(self):
            for d in (1, -1):
                for h in (0, 1):
                    self.c[h, "p1", d].wait_recv()
                    ref = slot(self.buf, h, -d, 0, self.parts[0 if d == 1 else 1])
                    self.c[h, "f1", d] = send(ref, ref, plane_dev(*at(h, d, 0)))
                    self.spread(h, 1 if d == 1 else 2)

        def forward(self, h, j):
            for d in (1, -1):
                self.c[h, j, d].wait_recv()
                ref = slot(self.buf, h, self.shifts[j], -d, self.parts[0 if d == 1 else 1])
                self.c[h, j, "f", d] = send(ref, ref, plane_dev(*at(h, 0, d)))

        def second_ring(self):
            for h in (0, 1):
                self.forward(h, 0)
            for h in (0, 1):
                self.c[h, "f1", 1].wait_recv()
                self.c[h, "f1", -1].wait_recv()
                self.spread(h, 3)
            for j in (1, 2, 3):
                for h in (0, 1):
                    self.forward(h, j)

        def finish(self):
            for j in range(4):
                for h in (0, 1):
                    for d in (1, -1):
                        self.c[h, j, "f", d].wait_recv()

    def to_plane(buf, row):
        buf[me_t] = row
        out = []
        for k in range(1, PLANE):
            ref = buf.at[me_t]
            out.append(send(ref, ref, (me_s, lax.rem(me_t + k, PLANE))))
        return out

    def to_line(buf, row):
        buf[me_s] = row
        out = []
        for k in range(1, LINE):
            ref = buf.at[me_s]
            out.append(send(ref, ref, (lax.rem(me_s + k, LINE), me_t)))
        return out

    def arrived(copies):
        for copy in copies:
            copy.wait_recv()

    def lse_over_first(a):
        top = jnp.max(a, axis=0)
        return top + jnp.log(jnp.sum(jnp.exp2(a - top[None]), axis=0)) * LOG2E

    def as_column(row, ref):
        for b in range(COLS // 128):
            piece = row[:, 128 * b : 128 * b + 128]
            ref[128 * b : 128 * b + 128, :] = jnp.broadcast_to(piece, (128, 128)).T

    def column_top(ref):
        return jnp.concatenate([ref[128 * b : 128 * b + 128, :].T[0:1, :] for b in range(COLS // 128)], axis=1)

    def column_sum(ref):
        return jnp.concatenate(
            [jnp.sum(ref[128 * b : 128 * b + 128, :].T, axis=0, keepdims=True) for b in range(COLS // 128)], axis=1
        )

    def tslot(dy, other, cols):
        k = wrap(y + dy) * 2 + (1 - core if other else core)
        return tg.at[pl.ds(pl.multiple_of(k * 32, 32), 32), cols]

    def line_dev(dy, other):
        return (wrap(y + dy) * 2 + (1 - core if other else core), me_t)

    all_cols = pl.ds(0, COLS)
    thalf = (pl.ds(0, COLS // 2), pl.ds(COLS // 2, COLS // 2))
    tcopy = {}
    for d in (1, -1):
        tcopy["y", d] = send(tgt, tslot(0, False, all_cols), line_dev(d, False))
    sgather = Gather(src, sg, 0, ROWS)
    tcopy["c", 0] = send(tgt, tslot(0, False, all_cols), line_dev(0, True))
    tg[pl.ds(pl.multiple_of(me_s * 32, 32), 32), :] = tgt[...]
    sg[pl.ds(pl.multiple_of(me_t * 16, 16), 16), :] = src[...]
    for d in (1, -1):
        tcopy["y", d].wait_recv()
        ref = tslot(-d, False, thalf[0 if d == 1 else 1])
        tcopy["f", d] = send(ref, ref, line_dev(d, False))
        ref = tslot(-d, False, all_cols)
        tcopy["c", -d] = send(ref, ref, line_dev(0, True))
    sgather.first_ring()
    tcopy["f", 1].wait_recv()
    tcopy["f", -1].wait_recv()
    ref = tslot(2, False, all_cols)
    tcopy["c", 2] = send(ref, ref, line_dev(0, True))
    sgather.second_ring()
    for d in (0, 1, -1, 2):
        tcopy["c", d].wait_recv()

    half_t = 0.5 * jnp.sum(tg[...] * tg[...], axis=0, keepdims=True)
    for b in range(COLS // 128):
        here = slice(128 * b, 128 * b + 128)
        high, low = halves(tg[:, here].T * SCALE)
        tcat[here, 0:256] = high
        tcat[here, 256:512] = high
        tcat[here, 512:768] = low
    as_column(half_t * SCALE, cb)

    sgather.finish()

    def split_points(buf, n, width):
        cols = pl.ds(pl.multiple_of(n * width, width), width)
        a = buf[:, cols]
        high, low = halves(a)
        scat[0:256, cols] = high
        scat[256:512, cols] = low
        scat[512:768, cols] = high
        return 0.5 * jnp.sum(a * a, axis=0, keepdims=True)

    WIDTH = 256

    def cross_step(n, _):
        cols = pl.ds(pl.multiple_of(n * WIDTH, WIDTH), WIDTH)
        frow[:, cols] = split_points(sg, n, WIDTH)
        cross = jnp.dot(tcat[...], scat[:, cols], preferred_element_type=F32)
        bias = cb[...]
        scores = cross - jnp.concatenate([bias, bias], axis=1)
        q[:, cols] = scores
        phi[:, cols] = jnp.max(scores, axis=0, keepdims=True)
        return 0

    lax.fori_loop(0, ROWS // WIDTH, cross_step, 0)

    def row_pass(body):
        def step(r, acc):
            return acc + body(pl.ds(pl.multiple_of(r * 8, 8), 8))

        acc = lax.fori_loop(0, COLS // 8, step, jnp.zeros((8, ROWS), F32), unroll=4)
        return jnp.sum(acc, axis=0, keepdims=True)

    top = phi[...]
    total = row_pass(lambda rows: jnp.exp2(q[rows, :] - top))
    copies = to_plane(vr.at[0], top + jnp.log(total) * LOG2E)
    arrived(copies)
    lse = lse_over_first(vr[0])
    phi[...] = slw[...] * LOG2E - lse
    frow[...] = frow[...] + EPSILON * (slw[...] - LN2 * lse)

    def col_pass(keep):
        def step(r, _):
            rows = pl.ds(pl.multiple_of(r * 8, 8), 8)
            scores = q[rows, :] + phi[...]
            top = jnp.max(scores, axis=1, keepdims=True)
            p = jnp.exp2(scores - top)
            if keep:
                e[rows, :] = p
            nb[rows, :] = jnp.broadcast_to(top, (8, 128))
            sb[rows, :] = functools.reduce(lambda a, b: a + b, [p[:, 128 * k : 128 * k + 128] for k in range(16)])
            return 0

        lax.fori_loop(0, COLS // 8, step, 0, unroll=4)
        return column_top(nb), column_sum(sb)

    ntop, total = col_pass(True)
    copies = to_line(vc.at[0], ntop + jnp.log(total) * LOG2E)
    arrived(copies)
    factor = jnp.exp2(ntop + (tlw[...] * LOG2E - lse_over_first(vc[0])))
    as_column(factor, cb)

    def against_column(rows):
        c = cb[rows, :]
        return e[rows, :] * jnp.concatenate([c] * 16, axis=1)

    copies = to_plane(vr.at[1], row_pass(against_column))
    arrived(copies)
    total = jnp.sum(vr[1], axis=0)
    f2 = frow[...] + EPSILON * (slw[...] - jnp.log(total))
    rowp[...] = f2
    phi[...] = jnp.exp(slw[...]) / total

    def weigh_step(r, _):
        rows = pl.ds(pl.multiple_of(r * 8, 8), 8)
        p = e[rows, :] * phi[...]
        sb[rows, :] = functools.reduce(lambda a, b: a + b, [p[:, 128 * k : 128 * k + 128] for k in range(16)])
        return 0

    lax.fori_loop(0, COLS // 8, weigh_step, 0, unroll=4)
    copies = to_line(vc.at[1], factor * column_sum(sb))
    arrived(copies)
    dual = factor * (jnp.exp(tlw[...]) / jnp.sum(vc[1], axis=0))
    as_column(dual, cb)

    copies = to_plane(vr.at[2], row_pass(against_column))
    high, low = halves(tg[...] * dual)
    tw[0:256, :] = high
    tw[256:512, :] = low
    BLOCK = 512
    for n in range(ROWS // BLOCK):
        cols = slice(n * BLOCK, n * BLOCK + BLOCK)

        def split_step(r, _):
            rows = pl.ds(pl.multiple_of(r * 16, 16), 16)
            high, low = halves(e[rows, cols])
            eh[rows, :] = high
            el[rows, :] = low
            return 0

        lax.fori_loop(0, COLS // 16, split_step, 0, unroll=4)
        acc = jnp.dot(tw[0:256, :], eh[...], preferred_element_type=F32)
        acc = acc + jnp.dot(tw[0:256, :], el[...], preferred_element_type=F32)
        acc = acc + jnp.dot(tw[256:512, :], eh[...], preferred_element_type=F32)
        w[:, :, :, :, cols] = acc.reshape(SIDE, SIDE, 2, 8, BLOCK)

    first_half, second_half = pl.ds(0, ROWS // 2), pl.ds(ROWS // 2, ROWS // 2)

    def group(h, shift):
        return (slice(None), wrap(z + shift), 0) if h == 0 else (wrap(x + shift), slice(None), 1)

    def single(h, shift):
        return (wrap(x + shift), z, 0) if h == 0 else (x, wrap(z + shift), 1)

    def cut(index, cols):
        return (*index, slice(None), cols)

    c = {}
    for h in (0, 1):
        for d, part in ((1, first_half), (-1, second_half)):
            c[h, "a", d] = send(w.at[cut(group(h, 2), part)], r1.at[h, :, :, part], plane_dev(*at(h, 0, d)))
    for h in (0, 1):
        for d, part in ((1, first_half), (-1, second_half)):
            c[h, "a", d].wait_recv()
            ref = w.at[cut(group(h, d), part)]
            ref[...] = ref[...] + r1[h, :, :, part]
            c[h, "b", d] = send(w.at[cut(group(h, d), pl.ds(0, ROWS))], r2.at[h, 0 if d == 1 else 1], plane_dev(*at(h, 0, d)))
    for h in (0, 1):
        c[h, "b", 1].wait_recv()
        c[h, "b", -1].wait_recv()
        ref = w.at[group(h, 0)]
        ref[...] = ref[...] + r2[h, 0] + r2[h, 1]
        for d, part in ((1, first_half), (-1, second_half)):
            c[h, "c", d] = send(w.at[cut(single(h, 2), part)], q1.at[h, :, part], plane_dev(*at(h, d, 0)))
    for h in (0, 1):
        for d, part in ((1, first_half), (-1, second_half)):
            c[h, "c", d].wait_recv()
            ref = w.at[cut(single(h, d), part)]
            ref[...] = ref[...] + q1[h, :, part]
            c[h, "d", d] = send(w.at[cut(single(h, d), pl.ds(0, ROWS))], q2.at[h, 0 if d == 1 else 1], plane_dev(*at(h, d, 0)))
    arrived(copies)
    ratio = tim[...] / jnp.sum(vr[2], axis=0)
    for h in (0, 1):
        c[h, "d", 1].wait_recv()
        c[h, "d", -1].wait_recv()
        share = w[single(h, 0)] + q2[h, 0] + q2[h, 1]
        moved[8 * h : 8 * h + 8, :] = (1.0 - tim[...]) * src[8 * h : 8 * h + 8, :] + ratio * share

    mgather = Gather(moved, mg, 0, ROWS)
    mg[pl.ds(pl.multiple_of(me_t * 16, 16), 16), :] = moved[...]
    mgather.first_ring()
    mgather.second_ring()
    mgather.finish()

    def last_step(n, _):
        cols = pl.ds(pl.multiple_of(n * WIDTH, WIDTH), WIDTH)
        phi[:, cols] = (rowp[:, cols] - split_points(mg, n, WIDTH)) * SCALE
        q[:, cols] = jnp.dot(tcat[...], scat[:, cols], preferred_element_type=F32)
        return 0

    lax.fori_loop(0, ROWS // WIDTH, last_step, 0)
    ntop, total = col_pass(False)
    copies = to_line(vc.at[2], ntop + jnp.log(total) * LOG2E)
    arrived(copies)
    colp[...] = EPSILON * (tlw[...] - LN2 * lse_over_first(vc[2])) + half_t

    for copy in started:
        copy.wait_send()


def per_device(sources, targets, source_logw, target_logw, times):
    vmem = pl.BlockSpec(memory_space=pltpu.VMEM)
    rowp, moved, colp = pl.pallas_call(
        kernel,
        out_shape=(
            jax.ShapeDtypeStruct((1, ROWS), F32),
            jax.ShapeDtypeStruct((16, ROWS), F32),
            jax.ShapeDtypeStruct((1, COLS), F32),
        ),
        in_specs=[vmem] * 5,
        out_specs=(vmem,) * 3,
        scratch_shapes=[
            pltpu.VMEM((FEATURES, ROWS), F32),
            pltpu.VMEM((FEATURES, COLS), F32),
            pltpu.VMEM((FEATURES, ROWS), F32),
            pltpu.VMEM((COLS, 3 * FEATURES), BF16),
            pltpu.VMEM((3 * FEATURES, ROWS), BF16),
            pltpu.VMEM((COLS, ROWS), F32),
            pltpu.VMEM((COLS, ROWS), F32),
            pltpu.VMEM((SIDE, SIDE, 2, 8, ROWS), F32),
            pltpu.VMEM((2 * FEATURES, COLS), BF16),
            pltpu.VMEM((COLS, 512), BF16),
            pltpu.VMEM((COLS, 512), BF16),
            pltpu.VMEM((2, SIDE, 8, ROWS), F32),
            pltpu.VMEM((2, 2, SIDE, 8, ROWS), F32),
            pltpu.VMEM((2, 8, ROWS), F32),
            pltpu.VMEM((2, 2, 8, ROWS), F32),
            pltpu.VMEM((3, PLANE, 1, ROWS), F32),
            pltpu.VMEM((3, LINE, 1, COLS), F32),
            pltpu.VMEM((COLS, 128), F32),
            pltpu.VMEM((COLS, 128), F32),
            pltpu.VMEM((COLS, 128), F32),
            pltpu.VMEM((1, ROWS), F32),
            pltpu.VMEM((1, ROWS), F32),
            pltpu.VMEM((1, ROWS), F32),
            pltpu.SemaphoreType.DMA((COPIES,)),
            pltpu.SemaphoreType.DMA((COPIES,)),
        ],
        compiler_params=pltpu.CompilerParams(
            collective_id=0, has_side_effects=True, vmem_limit_bytes=60 * 1024 * 1024
        ),
    )(sources, targets, source_logw[None], target_logw[None], times[None])
    return rowp[0], moved, colp[0]


def solution(mesh):
    return jax.shard_map(
        per_device,
        mesh=mesh,
        in_specs=(P("tgt", "src"), P("src", "tgt"), P("src"), P("tgt"), P("src")),
        out_specs=(P("src"), P("tgt", "src"), P("tgt")),
        check_vma=False,
    )
```

```python
import functools

import jax
import jax.numpy as jnp
from jax import lax
from jax.experimental import pallas as pl
from jax.experimental.pallas import tpu as pltpu
from jax.sharding import PartitionSpec as P

MESH = pl.DeviceIdType.MESH
F32 = jnp.float32
BF16 = jnp.bfloat16
EPSILON = 16.0
LOG2E = 1.4426950408889634
LN2 = 0.6931471805599453
SCALE = LOG2E / EPSILON

FEATURES = 256
ROWS = 2048
COLS = 1024
SIDE = 4
GROUP = 16
LINE = 8
COPIES = 256
CHUNKS = 2
CHUNK = ROWS // CHUNKS
WIDTH = 256


def halves(a):
    high = a.astype(BF16)
    return high, (a - high.astype(F32)).astype(BF16)


def tiles(a):
    return functools.reduce(lambda p, r: p + r, [a[:, 128 * k : 128 * k + 128] for k in range(ROWS // 128)])


def kernel(
    src_h, tgt_h, slw_h, tlw_h, tim_h,
    rowp, moved, colp,
    src, tgt, own, far, slw, tlw, tim, sg, tg, mg, mv, tcat, scat, q, e, w, tw, eh, el,
    r0, rb, rx1, rx2, qb, vr, vc, nb, sb, cb, part, frow, phi, f2, ff,
    send_sem, recv_sem, in_sem,
):
    me_s, me_t = lax.axis_index("src"), lax.axis_index("tgt")
    x, z = me_t // SIDE, me_t % SIDE
    y, core = me_s // 2, me_s % 2
    block = z // 2
    mate = z + 1 - 2 * (z % 2)
    opp = SIDE - 1 - z
    other = 1 - core
    mine = core == block
    started = []

    def wrap(value):
        return lax.rem(value + SIDE, SIDE)

    def dev(dx=0, dy=0, zz=z, cc=core):
        return (wrap(y + dy) * 2 + cc, wrap(x + dx) * SIDE + zz)

    def copy_to(source, target, device, k):
        return pltpu.make_async_remote_copy(
            src_ref=source, dst_ref=target, send_sem=send_sem.at[k], recv_sem=recv_sem.at[k],
            device_id=device, device_id_type=MESH,
        )

    count = [0]

    def number():
        count[0] += 1
        return count[0] - 1

    def send(source, target, device):
        copy = copy_to(source, target, device, number())
        copy.start()
        started.append(copy)
        return copy

    loads = [
        pltpu.make_async_copy(a, b, in_sem.at[k])
        for k, (a, b) in enumerate(((src_h, src), (tgt_h, tgt), (slw_h, own.at[0]), (tim_h, own.at[1]), (tlw_h, own.at[2, :, pl.ds(0, COLS)])))
    ]
    for load in loads:
        load.start()
    barrier = pltpu.get_barrier_semaphore()
    near = [dev(1), dev(-1), dev(dy=1), dev(dy=-1), dev(zz=mate), dev(zz=opp), dev(zz=opp, cc=other), dev(cc=other)]
    for device in near:
        pl.semaphore_signal(barrier, inc=1, device_id=device, device_id_type=MESH)
    for load in loads:
        load.wait()
    pl.semaphore_wait(barrier, len(near))

    def slot(buf, dx, zz, cc, cols):
        return buf.at[pl.ds(pl.multiple_of((wrap(x + dx) * SIDE + zz) * 16 + 8 * cc, 8), 8), cols]

    def chunk_cols(n):
        return pl.ds(n * CHUNK, CHUNK)

    def chunk_half(n, d):
        return pl.ds(n * CHUNK + (0 if d == 1 else CHUNK // 2), CHUNK // 2)

    class Gather:
        def __init__(self, buf, n):
            self.buf, self.n = buf, n
            self.cols = chunk_cols(n)
            self.c = {}
            self.local = []

        def share(self, dx, zz):
            ref = slot(self.buf, dx, zz, core, self.cols)
            self.local.append(send(ref, ref, dev(cc=other)))

        def to_mate(self, key, dx, zz):
            ref = slot(self.buf, dx, zz, core, self.cols)
            self.c[key] = send(ref, ref, dev(zz=mate))

        def round_x(self, key, zz):
            ref = slot(self.buf, 0, zz, core, self.cols)
            for d in (1, -1):
                self.c[key, d] = send(ref, ref, dev(d))

        def onward(self, key, zz):
            for d in (1, -1):
                self.c[key, d].wait_recv()
                ref = slot(self.buf, -d, zz, core, chunk_half(self.n, d))
                self.c[key, "f", d] = send(ref, ref, dev(d))

        def end_of_round(self, key):
            for d in (1, -1):
                self.c[key, "f", d].wait_recv()

        def start_near(self):
            self.round_x("n", z)
            self.to_mate(("m", 0), 0, z)
            self.share(0, z)

        def start_far(self):
            self.to_mate("fm", 0, opp)
            self.round_x("f", opp)
            self.share(0, opp)

        def step1(self):
            self.onward("n", z)
            for d in (1, -1):
                self.to_mate(("m", -d), -d, z)
                self.share(-d, z)

        def step2(self):
            self.c["fm"].wait_recv()
            self.round_x("g", SIDE - 1 - mate)
            self.share(0, SIDE - 1 - mate)
            self.onward("f", opp)
            for d in (1, -1):
                self.share(-d, opp)

        def step3(self):
            self.end_of_round("n")
            self.to_mate(("m", 2), 2, z)
            self.share(2, z)
            self.c["m", 0].wait_recv()
            self.share(0, mate)
            self.onward("g", SIDE - 1 - mate)
            for d in (1, -1):
                self.share(-d, SIDE - 1 - mate)

        def step4(self):
            self.end_of_round("f")
            self.share(2, opp)
            for d in (1, -1, 2):
                self.c["m", d].wait_recv()
                self.share(d, mate)
            self.end_of_round("g")
            self.share(2, SIDE - 1 - mate)

        def finish(self):
            for copy in self.local:
                copy.wait_recv()

    def group_devices():
        return [
            dev(dx, zz=zz, cc=cc)
            for dx in (2, 1, -1, 0)
            for zz in (mate, z)
            for cc in (other, core)
            if not (dx == 0 and zz is z and cc is core)
        ]

    group_slot = x * 4 + (z % 2) * 2 + core
    line_slot = y * 2 + block

    def to_all(buf, k, row, devices):
        buf[k] = row
        return [send(buf.at[k], buf.at[k], device) for device in devices]

    def to_group(buf, row):
        return to_all(buf, group_slot, row, group_devices())

    line = [(dy, zz, cc) for dy in (2, 1, -1, 0) for zz, cc in ((opp, other), (z, core)) if not (dy == 0 and zz is z)]

    def to_line(buf, row):
        return to_all(buf, line_slot, row, [dev(dy=dy, zz=zz, cc=cc) for dy, zz, cc in line])

    def arrived(copies):
        for copy in copies:
            copy.wait_recv()

    def lse_over_first(a):
        top = jnp.max(a, axis=0)
        return top + jnp.log(jnp.sum(jnp.exp2(a - top[None]), axis=0)) * LOG2E

    def as_column(row, ref):
        for b in range(COLS // 128):
            piece = row[:, 128 * b : 128 * b + 128]
            ref[128 * b : 128 * b + 128, :] = jnp.broadcast_to(piece, (128, 128)).T

    def column_top(ref):
        return jnp.concatenate([ref[128 * b : 128 * b + 128, :].T[0:1, :] for b in range(COLS // 128)], axis=1)

    def column_sum(ref):
        return jnp.concatenate(
            [jnp.sum(ref[128 * b : 128 * b + 128, :].T, axis=0, keepdims=True) for b in range(COLS // 128)], axis=1
        )

    both = pl.ds(0, ROWS)
    k_near = number()
    k_far = (number(), number())

    def out_half(cc):
        return src.at[pl.ds(pl.multiple_of(8 * cc, 8), 8), :]

    give_near = copy_to(out_half(other), slot(sg, 0, z, other, both), dev(cc=other), k_near)
    give_far = [copy_to(out_half(0), slot(sg, 0, z, 0, both), dev(zz=opp, cc=0), k_far[0]), None]
    take_near = copy_to(out_half(0), slot(sg, 0, z, core, both), dev(cc=other), k_near)
    take_far = copy_to(out_half(0), slot(sg, 0, opp, core, both), dev(zz=opp), k_far[0])
    give_far[1] = pltpu.make_async_remote_copy(
        src_ref=out_half(1), dst_ref=slot(sg, 0, z, 1, both), send_sem=send_sem.at[k_far[1]], recv_sem=recv_sem.at[k_far[0]],
        device_id=dev(zz=opp, cc=1), device_id_type=MESH,
    )

    k_t = (number(), number())

    def tslot(dy, cc, rows=None):
        start, size = (0, 32) if rows is None else rows
        return tg.at[pl.ds(pl.multiple_of(64 * wrap(y + dy) + 32 * cc + start, 16), size), :]

    def tcopy(device, k):
        return pltpu.make_async_remote_copy(
            src_ref=tgt, dst_ref=tslot(0, core), send_sem=send_sem.at[k], recv_sem=recv_sem.at[k_t[0] + core],
            device_id=device, device_id_type=MESH,
        )

    give_t = tcopy(dev(zz=opp, cc=1), k_t[0])
    give_t_here = tcopy(dev(cc=0), k_t[1])
    take_t = [copy_to(tgt, tslot(0, cc), dev(zz=opp, cc=1), k_t[cc]) for cc in (0, 1)]

    give_t.start()

    @pl.when(core == 1)
    def _():
        give_t_here.start()

    @pl.when(mine)
    def _():
        give_near.start()

    @pl.when(jnp.logical_not(mine))
    def _():
        give_far[0].start()
        give_far[1].start()

    small = [
        send(own.at[0], far.at[0], dev(cc=other)),
        send(own.at[1], far.at[1], dev(cc=other)),
        send(own.at[2, :, pl.ds(0, COLS)], far.at[2, :, pl.ds(0, COLS)], dev(zz=opp)),
    ]

    @pl.when(mine)
    def _():
        slot(sg, 0, z, core, both)[...] = out_half(core)[...]

    @pl.when(core == 0)
    def _():
        tslot(0, 0)[...] = tgt[...]

    @pl.when(jnp.logical_not(mine))
    def _():
        take_near.wait_recv()

    gathers = [Gather(sg, n) for n in range(CHUNKS)]
    for g in gathers:
        g.start_near()

    @pl.when(core == 1)
    def _():
        take_t[0].wait_recv()

    yc = {}
    for cc in (0, 1):
        if cc == 1:
            take_t[1].wait_recv()
        for d in (1, -1):
            yc[cc, d] = send(tslot(0, cc), tslot(0, cc), dev(dy=d))
    take_far.wait_recv()
    for g in gathers:
        g.start_far()
    gathers[0].step1()
    for cc in (0, 1):
        for d in (1, -1):
            yc[cc, d].wait_recv()
            ref = tslot(-d, cc, (0 if d == 1 else 16, 16))
            yc[cc, "f", d] = send(ref, ref, dev(dy=d))
    for g in gathers[1:]:
        g.step1()
    for g in gathers:
        g.step2()
    for g in gathers[:-1]:
        g.step3()
    for cc in (0, 1):
        for d in (1, -1):
            yc[cc, "f", d].wait_recv()

    half_t = 0.5 * jnp.sum(tg[...] * tg[...], axis=0, keepdims=True)
    for b in range(COLS // 128):
        here = slice(128 * b, 128 * b + 128)
        high, low = halves(tg[:, here].T * SCALE)
        tcat[here, 0:256] = high
        tcat[here, 256:512] = high
        tcat[here, 512:768] = low
    as_column(half_t * SCALE, cb)

    gathers[-1].step3()
    for g in gathers[:-1]:
        g.step4()

    def split_points(buf, n):
        cols = pl.ds(pl.multiple_of(n * WIDTH, WIDTH), WIDTH)
        a = buf[:, cols]
        high, low = halves(a)
        scat[0:256, cols] = high
        scat[256:512, cols] = low
        scat[512:768, cols] = high
        return 0.5 * jnp.sum(a * a, axis=0, keepdims=True)

    def cross_step(n, _):
        cols = pl.ds(pl.multiple_of(n * WIDTH, WIDTH), WIDTH)
        frow[:, cols] = split_points(sg, n)
        cross = jnp.dot(tcat[...], scat[:, cols], preferred_element_type=F32)
        bias = cb[...]
        scores = cross - jnp.concatenate([bias, bias], axis=1)
        q[:, cols] = scores
        phi[:, cols] = jnp.max(scores, axis=0, keepdims=True)
        return 0

    def over_chunk(n, step):
        lax.fori_loop(n * CHUNK // WIDTH, (n + 1) * CHUNK // WIDTH, step, 0)

    for n, g in enumerate(gathers):
        if n == CHUNKS - 1:
            g.step4()
        g.finish()
        over_chunk(n, cross_step)

    arrived(small)
    slw[...] = jnp.where(mine, own[0], far[0])
    tim[...] = jnp.where(mine, own[1], far[1])
    tlw[...] = jnp.where(core == 0, own[2], far[2])[:, 0:COLS]

    give_t.wait_send()

    @pl.when(core == 1)
    def _():
        give_t_here.wait_send()

    @pl.when(mine)
    def _():
        give_near.wait_send()

    @pl.when(jnp.logical_not(mine))
    def _():
        give_far[0].wait_send()
        give_far[1].wait_send()

    def row_pass(body):
        def step(r, acc):
            return acc + body(pl.ds(pl.multiple_of(r * 8, 8), 8))

        acc = lax.fori_loop(0, COLS // 8, step, jnp.zeros((8, ROWS), F32), unroll=4)
        return jnp.sum(acc, axis=0, keepdims=True)

    top = phi[...]
    total = row_pass(lambda rows: jnp.exp2(q[rows, :] - top))
    copies = to_group(vr.at[0], top + jnp.log(total) * LOG2E)
    arrived(copies)
    lse = lse_over_first(vr[0])
    phi[...] = slw[...] * LOG2E - lse
    frow[...] = frow[...] + EPSILON * (slw[...] - LN2 * lse)

    def col_pass(keep):
        def top_step(r, _):
            rows = pl.ds(pl.multiple_of(r * 8, 8), 8)
            scores = q[rows, :] + phi[...]
            nb[rows, :] = functools.reduce(jnp.maximum, [scores[:, 128 * k : 128 * k + 128] for k in range(ROWS // 128)])
            return 0

        lax.fori_loop(0, COLS // 8, top_step, 0, unroll=4)

        def join_step(r, _):
            rows = pl.ds(pl.multiple_of(r * 128, 128), 128)
            nb[rows, :] = jnp.broadcast_to(jnp.max(nb[rows, :], axis=1, keepdims=True), (128, 128))
            return 0

        lax.fori_loop(0, COLS // 128, join_step, 0)

        def step(r, _):
            rows = pl.ds(pl.multiple_of(r * 8, 8), 8)
            p = jnp.exp2(q[rows, :] + phi[...] - jnp.concatenate([nb[rows, :]] * (ROWS // 128), axis=1))
            if keep:
                e[rows, :] = p
            sb[rows, :] = tiles(p)
            return 0

        lax.fori_loop(0, COLS // 8, step, 0, unroll=4)
        return column_top(nb), column_sum(sb)

    ntop, total = col_pass(True)
    copies = to_line(vc.at[0], ntop + jnp.log(total) * LOG2E)
    arrived(copies)
    factor = jnp.exp2(ntop + (tlw[...] * LOG2E - lse_over_first(vc[0])))
    as_column(factor, cb)

    def against_column(rows):
        return e[rows, :] * jnp.concatenate([cb[rows, :]] * (ROWS // 128), axis=1)

    copies = to_group(vr.at[1], row_pass(against_column))
    arrived(copies)
    total = jnp.sum(vr[1], axis=0)
    f2[...] = frow[...] + EPSILON * (slw[...] - jnp.log(total))
    phi[...] = jnp.exp(slw[...]) / total
    potential = send(f2, ff, dev(zz=opp))

    def weigh_step(r, _):
        rows = pl.ds(pl.multiple_of(r * 8, 8), 8)
        sb[rows, :] = tiles(e[rows, :] * phi[...])
        return 0

    lax.fori_loop(0, COLS // 8, weigh_step, 0, unroll=4)
    copies = to_line(vc.at[1], factor * column_sum(sb))
    arrived(copies)
    dual = factor * (jnp.exp(tlw[...]) / jnp.sum(vc[1], axis=0))
    as_column(dual, cb)

    potential.wait_recv()

    copies = to_group(vr.at[2], row_pass(against_column))
    high, low = halves(tg[...] * dual)
    tw[0:256, :] = high
    tw[256:512, :] = low
    BLOCK = 512

    def wz(zz, cols, dx=None):
        return w.at[slice(None) if dx is None else wrap(x + dx), zz, core, :, cols]

    mates_opp = SIDE - 1 - mate
    c = {}
    for n in range(CHUNKS):
        for m in range(n * CHUNK // BLOCK, (n + 1) * CHUNK // BLOCK):
            cols = slice(m * BLOCK, m * BLOCK + BLOCK)

            def split_step(r, _):
                rows = pl.ds(pl.multiple_of(r * 16, 16), 16)
                high, low = halves(e[rows, cols])
                eh[rows, :] = high
                el[rows, :] = low
                return 0

            lax.fori_loop(0, COLS // 16, split_step, 0, unroll=4)
            acc = jnp.dot(tw[0:256, :], eh[...], preferred_element_type=F32)
            acc = acc + jnp.dot(tw[0:256, :], el[...], preferred_element_type=F32)
            acc = acc + jnp.dot(tw[256:512, :], eh[...], preferred_element_type=F32)
            w[:, :, :, :, cols] = acc.reshape(SIDE, SIDE, 2, 8, BLOCK)
        cols = chunk_cols(n)
        c[n, "core"] = send(w.at[:, :, other, :, cols], r0.at[:, :, :, cols], dev(cc=other))

    def rx_start(n, key, zz, k):
        for d in (1, -1):
            cut = chunk_half(n, d)
            c[n, key, d] = send(wz(zz, cut, 2), rx1.at[k, :, cut], dev(d))

    def rx_middle(n, key, zz, k):
        for d in (1, -1):
            cut = chunk_half(n, d)
            c[n, key, d].wait_recv()
            ref = wz(zz, cut, d)
            ref[...] = ref[...] + rx1[k, :, cut]
            c[n, key, "s", d] = send(wz(zz, chunk_cols(n), d), rx2.at[k, 0 if d == 1 else 1, :, chunk_cols(n)], dev(d))

    def rx_end(n, key, zz, k):
        for d in (1, -1):
            c[n, key, "s", d].wait_recv()
        cols = chunk_cols(n)
        return wz(zz, cols, 0)[...] + rx2[k, 0, :, cols] + rx2[k, 1, :, cols]

    def rs1(n):
        cols = chunk_cols(n)
        c[n, "core"].wait_recv()
        ref = w.at[:, :, core, :, cols]
        ref[...] = ref[...] + r0[:, :, :, cols]
        c[n, "mate"] = send(wz(mate, cols), rb.at[:, :, cols], dev(zz=mate))
        rx_start(n, "m", mates_opp, 0)
        rx_start(n, "o", opp, 1)

    def rs2(n):
        cols = chunk_cols(n)
        rx_middle(n, "m", mates_opp, 0)
        c[n, "mate"].wait_recv()
        ref = wz(z, cols)
        ref[...] = ref[...] + rb[:, :, cols]
        rx_start(n, "z", z, 2)
        rx_middle(n, "o", opp, 1)

    def rs3(n):
        cols = chunk_cols(n)
        qs = wz(mates_opp, cols, 0)
        qs[...] = rx_end(n, "m", mates_opp, 0)
        c[n, "last"] = send(qs, qb.at[:, cols], dev(zz=mate))
        rx_middle(n, "z", z, 2)

    def point_rows(zz):
        return pl.ds(pl.multiple_of((x * SIDE + zz) * 16 + 8 * core, 8), 8)

    mgathers = [Gather(mg, n) for n in range(CHUNKS)]
    k_out = [(number(), number()) for _ in range(CHUNKS)]
    outs = []

    def rs4(n):
        cols = chunk_cols(n)
        g = mgathers[n]
        ratio = tim[:, cols] / jnp.sum(vr[2, :, :, cols], axis=0)
        keep = 1.0 - tim[:, cols]
        share = rx_end(n, "o", opp, 1)
        c[n, "last"].wait_recv()
        mg[point_rows(opp), cols] = keep * sg[point_rows(opp), cols] + ratio * (share + qb[:, cols])
        g.start_far()
        share = rx_end(n, "z", z, 2)
        mg[point_rows(z), cols] = keep * sg[point_rows(z), cols] + ratio * share
        g.start_near()
        here = mv.at[pl.ds(pl.multiple_of(8 * core, 8), 8), cols]
        there = mv.at[pl.ds(pl.multiple_of(8 * other, 8), 8), cols]

        def result(zz, device, k):
            return pltpu.make_async_remote_copy(
                src_ref=slot(mg, 0, zz, core, cols), dst_ref=here, send_sem=send_sem.at[k], recv_sem=recv_sem.at[k_out[n][0] + core],
                device_id=device, device_id_type=MESH,
            )

        far_out = result(opp, dev(zz=opp, cc=block), k_out[n][0])
        near_out = result(z, dev(cc=other), k_out[n][1])
        far_out.start()
        started.append(far_out)

        @pl.when(mine)
        def _():
            here[...] = mg[point_rows(z), cols]

        @pl.when(jnp.logical_not(mine))
        def _():
            near_out.start()

        def result_in(ref, k):
            return pltpu.make_async_remote_copy(
                src_ref=ref, dst_ref=ref, send_sem=send_sem.at[k_out[n][0]], recv_sem=recv_sem.at[k],
                device_id=dev(cc=other), device_id_type=MESH,
            )

        outs.append((near_out, result_in(here, k_out[n][0] + core), result_in(there, k_out[n][0] + other)))

    order = [rs1, rs2, rs3]
    for stage in order:
        for n in range(CHUNKS):
            stage(n)
    arrived(copies)
    for n in range(CHUNKS):
        rs4(n)

    def last_step(n, _):
        cols = pl.ds(pl.multiple_of(n * WIDTH, WIDTH), WIDTH)
        phi[:, cols] = (f2[:, cols] - split_points(mg, n)) * SCALE
        q[:, cols] = jnp.dot(tcat[...], scat[:, cols], preferred_element_type=F32)
        return 0

    for name in ("step1", "step2", "step3"):
        for g in mgathers:
            getattr(g, name)()
    for n, g in enumerate(mgathers):
        g.step4()
        g.finish()
        over_chunk(n, last_step)
    ntop, total = col_pass(False)
    home = z + core * (opp - z)
    part[...] = ntop + jnp.log(total) * LOG2E - half_t * SCALE

    def to_owner(dy, cc, k, base):
        return pltpu.make_async_remote_copy(
            src_ref=part, dst_ref=vc.at[2, line_slot], send_sem=send_sem.at[k], recv_sem=recv_sem.at[base + core],
            device_id=dev(dy=dy, zz=home, cc=cc), device_id_type=MESH,
        )

    def from_owner(k):
        return copy_to(part, vc.at[2, line_slot], dev(cc=other), k)

    waits = []
    for dy in (2, 1, -1):
        base, more = number(), number()
        for cc, k in ((0, base), (1, more)):
            copy = to_owner(dy, cc, k, base)
            copy.start()
            started.append(copy)
        waits += [from_owner(base), from_owner(more)]
    base, more = number(), number()
    to_one, to_zero = to_owner(0, 1, more, base), to_owner(0, 0, base, base)
    to_one.start()
    started.append(to_one)

    @pl.when(core == 1)
    def _():
        to_zero.start()
        from_owner(base).wait_recv()

    @pl.when(core == 0)
    def _():
        vc[2, line_slot] = part[...]

    from_owner(more).wait_recv()
    arrived(waits)
    colp[...] = EPSILON * (own[2][:, 0:COLS] - LN2 * lse_over_first(vc[2]))

    rowp[...] = jnp.where(mine, f2[...], ff[...])
    for near_out, half_here, half_there in outs:
        half_there.wait_recv()

        @pl.when(jnp.logical_not(mine))
        def _():
            half_here.wait_recv()
            near_out.wait_send()

    moved[...] = mv[...]

    @pl.when(core == 1)
    def _():
        to_zero.wait_send()

    for copy in started:
        copy.wait_send()


def per_device(sources, targets, source_logw, target_logw, times):
    vmem, anywhere = pl.BlockSpec(memory_space=pltpu.VMEM), pl.BlockSpec(memory_space=pl.ANY)
    rowp, moved, colp = pl.pallas_call(
        kernel,
        out_shape=(
            jax.ShapeDtypeStruct((1, ROWS), F32),
            jax.ShapeDtypeStruct((16, ROWS), F32),
            jax.ShapeDtypeStruct((1, COLS), F32),
        ),
        in_specs=[anywhere] * 5,
        out_specs=(vmem,) * 3,
        scratch_shapes=[
            pltpu.VMEM((16, ROWS), F32),
            pltpu.VMEM((32, COLS), F32),
            pltpu.VMEM((3, 1, ROWS), F32),
            pltpu.VMEM((3, 1, ROWS), F32),
            pltpu.VMEM((1, ROWS), F32),
            pltpu.VMEM((1, COLS), F32),
            pltpu.VMEM((1, ROWS), F32),
            pltpu.VMEM((FEATURES, ROWS), F32),
            pltpu.VMEM((FEATURES, COLS), F32),
            pltpu.VMEM((FEATURES, ROWS), F32),
            pltpu.VMEM((16, ROWS), F32),
            pltpu.VMEM((COLS, 3 * FEATURES), BF16),
            pltpu.VMEM((3 * FEATURES, ROWS), BF16),
            pltpu.VMEM((COLS, ROWS), F32),
            pltpu.VMEM((COLS, ROWS), F32),
            pltpu.VMEM((SIDE, SIDE, 2, 8, ROWS), F32),
            pltpu.VMEM((2 * FEATURES, COLS), BF16),
            pltpu.VMEM((COLS, 512), BF16),
            pltpu.VMEM((COLS, 512), BF16),
            pltpu.VMEM((SIDE, SIDE, 8, ROWS), F32),
            pltpu.VMEM((SIDE, 8, ROWS), F32),
            pltpu.VMEM((3, 8, ROWS), F32),
            pltpu.VMEM((3, 2, 8, ROWS), F32),
            pltpu.VMEM((8, ROWS), F32),
            pltpu.VMEM((3, GROUP, 1, ROWS), F32),
            pltpu.VMEM((3, LINE, 1, COLS), F32),
            pltpu.VMEM((COLS, 128), F32),
            pltpu.VMEM((COLS, 128), F32),
            pltpu.VMEM((COLS, 128), F32),
            pltpu.VMEM((1, COLS), F32),
            pltpu.VMEM((1, ROWS), F32),
            pltpu.VMEM((1, ROWS), F32),
            pltpu.VMEM((1, ROWS), F32),
            pltpu.VMEM((1, ROWS), F32),
            pltpu.SemaphoreType.DMA((COPIES,)),
            pltpu.SemaphoreType.DMA((COPIES,)),
            pltpu.SemaphoreType.DMA((5,)),
        ],
        compiler_params=pltpu.CompilerParams(
            collective_id=0, has_side_effects=True, vmem_limit_bytes=60 * 1024 * 1024
        ),
    )(sources, targets, source_logw[None], target_logw[None], times[None])
    return rowp[0], moved, colp[0]


def solution(mesh):
    return jax.shard_map(
        per_device,
        mesh=mesh,
        in_specs=(P("tgt", "src"), P("src", "tgt"), P("src"), P("tgt"), P("src")),
        out_specs=(P("src"), P("tgt", "src"), P("tgt")),
        check_vma=False,
    )
```

```python
import functools

import jax
import jax.numpy as jnp
from jax import lax
from jax.experimental import pallas as pl
from jax.experimental.pallas import tpu as pltpu
from jax.sharding import PartitionSpec as P

MESH = pl.DeviceIdType.MESH
F32 = jnp.float32
BF16 = jnp.bfloat16
EPSILON = 16.0
LOG2E = 1.4426950408889634
LN2 = 0.6931471805599453
SCALE = LOG2E / EPSILON

FEATURES = 256
ROWS = 2048
COLS = 1024
SIDE = 4
GROUP = 16
LINE = 8
COPIES = 256
CHUNKS = 2
CHUNK = ROWS // CHUNKS
WIDTH = 256
PARTS = 2
PART = COLS // PARTS
BLOCK = 512


def halves(a):
    high = a.astype(BF16)
    return high, (a - high.astype(F32)).astype(BF16)


def tiles(a):
    return functools.reduce(lambda p, r: p + r, [a[:, 128 * k : 128 * k + 128] for k in range(a.shape[1] // 128)])


def kernel(
    src_h, tgt_h, slw_h, tlw_h, tim_h,
    rowp, moved, colp,
    src, tgt, own, far, slw, tlw, tim, sg, tg, mg, mv, tcat, scat, q, e, w, tw, eh, el,
    r0, rb, rx1, rx2, rd, qb, vr, vc, nb, sb, cb, part, frow, phi, f2, ff, fr, fc, half_t,
    send_sem, recv_sem, in_sem,
):
    me_s, me_t = lax.axis_index("src"), lax.axis_index("tgt")
    x, z = me_t // SIDE, me_t % SIDE
    y, core = me_s // 2, me_s % 2
    block = z // 2
    mate = z + 1 - 2 * (z % 2)
    opp = SIDE - 1 - z
    mates_opp = SIDE - 1 - mate
    other = 1 - core
    mine = core == block
    started = []

    def wrap(value):
        return lax.rem(value + SIDE, SIDE)

    def dev(dx=0, dy=0, zz=z, cc=core):
        return (wrap(y + dy) * 2 + cc, wrap(x + dx) * SIDE + zz)

    def copy_to(source, target, device, k):
        return pltpu.make_async_remote_copy(
            src_ref=source, dst_ref=target, send_sem=send_sem.at[k], recv_sem=recv_sem.at[k],
            device_id=device, device_id_type=MESH,
        )

    count = [0]

    def number():
        count[0] += 1
        return count[0] - 1

    def send(source, target, device):
        copy = copy_to(source, target, device, number())
        copy.start()
        started.append(copy)
        return copy

    loads = [
        pltpu.make_async_copy(a, b, in_sem.at[k])
        for k, (a, b) in enumerate(((src_h, src), (tgt_h, tgt), (slw_h, own.at[0]), (tim_h, own.at[1]), (tlw_h, own.at[2, :, pl.ds(0, COLS)])))
    ]
    for load in loads:
        load.start()
    stores = [pltpu.make_async_copy(a, b, in_sem.at[k]) for k, (a, b) in enumerate(((mv, moved), (fr, rowp), (fc, colp)))]
    barrier = pltpu.get_barrier_semaphore()
    near = [dev(1), dev(-1), dev(2), dev(dy=1), dev(dy=-1), dev(zz=mate), dev(zz=opp), dev(zz=opp, cc=other), dev(cc=other)]
    for device in near:
        pl.semaphore_signal(barrier, inc=1, device_id=device, device_id_type=MESH)
    for load in loads:
        load.wait()
    pl.semaphore_wait(barrier, len(near))

    def slot(buf, dx, zz, cc, cols):
        return buf.at[pl.ds(pl.multiple_of((wrap(x + dx) * SIDE + zz) * 16 + 8 * cc, 8), 8), cols]

    def chunk_cols(n):
        return pl.ds(n * CHUNK, CHUNK)

    def chunk_half(n, d):
        return pl.ds(n * CHUNK + (0 if d == 1 else CHUNK // 2), CHUNK // 2)

    class Gather:
        def __init__(self, buf, n):
            self.buf, self.n = buf, n
            self.cols = chunk_cols(n)
            self.c = {}
            self.local = []

        def share(self, dx, zz):
            ref = slot(self.buf, dx, zz, core, self.cols)
            self.local.append(send(ref, ref, dev(cc=other)))

        def to_mate(self, key, dx, zz):
            ref = slot(self.buf, dx, zz, core, self.cols)
            self.c[key] = send(ref, ref, dev(zz=mate))

        def round_x(self, key, zz, shifts):
            ref = slot(self.buf, 0, zz, core, self.cols)
            for d in shifts:
                self.c[key, d] = send(ref, ref, dev(d))

        def near(self):
            self.round_x("n", z, (2, 1, -1))
            self.to_mate(("m", 0), 0, z)
            self.share(0, z)

        def far(self):
            self.to_mate("fm", 0, opp)
            self.share(0, opp)

        def far_x(self):
            self.round_x("f", opp, (1, -1))

        def near_on(self):
            for d in (1, -1, 2):
                self.c["n", d].wait_recv()
                self.to_mate(("m", -d), -d, z)
                self.share(-d, z)

        def far_on(self):
            self.c["fm"].wait_recv()
            self.round_x("g", mates_opp, (2, 1, -1))
            self.share(0, mates_opp)
            for d in (1, -1):
                self.c["f", d].wait_recv()
                ref = slot(self.buf, -d, opp, core, chunk_half(self.n, d))
                self.c["ff", d] = send(ref, ref, dev(d))
                self.share(-d, opp)

        def last(self):
            self.c["m", 0].wait_recv()
            self.share(0, mate)
            for d in (1, -1):
                self.c["ff", d].wait_recv()
            self.share(2, opp)
            for d in (1, -1, 2):
                self.c["m", -d].wait_recv()
                self.share(-d, mate)
                self.c["g", d].wait_recv()
                self.share(-d, mates_opp)

        def finish(self):
            for copy in self.local:
                copy.wait_recv()

    def group_devices():
        return [
            dev(dx, zz=zz, cc=cc)
            for dx in (2, 1, -1, 0)
            for zz in (mate, z)
            for cc in (other, core)
            if not (dx == 0 and zz is z and cc is core)
        ]

    group_slot = x * 4 + (z % 2) * 2 + core
    line_slot = y * 2 + block

    def to_all(buf, k, row, devices):
        buf[k] = row
        return [send(buf.at[k], buf.at[k], device) for device in devices]

    def to_group(buf, row):
        return to_all(buf, group_slot, row, group_devices())

    line = [(dy, zz, cc) for dy in (2, 1, -1, 0) for zz, cc in ((opp, other), (z, core)) if not (dy == 0 and zz is z)]

    def to_line(buf, row):
        return to_all(buf, line_slot, row, [dev(dy=dy, zz=zz, cc=cc) for dy, zz, cc in line])

    def arrived(copies):
        for copy in copies:
            copy.wait_recv()

    def lse_over_first(a):
        top = jnp.max(a, axis=0)
        return top + jnp.log(jnp.sum(jnp.exp2(a - top[None]), axis=0)) * LOG2E

    def as_column(row, ref):
        for b in range(COLS // 128):
            piece = row[:, 128 * b : 128 * b + 128]
            ref[128 * b : 128 * b + 128, :] = jnp.broadcast_to(piece, (128, 128)).T

    def column_top(ref):
        return jnp.concatenate([ref[128 * b : 128 * b + 128, :].T[0:1, :] for b in range(COLS // 128)], axis=1)

    def column_sum(ref):
        return jnp.concatenate(
            [jnp.sum(ref[128 * b : 128 * b + 128, :].T, axis=0, keepdims=True) for b in range(COLS // 128)], axis=1
        )

    both = pl.ds(0, ROWS)
    k_near = number()
    k_far = (number(), number())

    def out_half(cc):
        return src.at[pl.ds(pl.multiple_of(8 * cc, 8), 8), :]

    give_near = copy_to(out_half(other), slot(sg, 0, z, other, both), dev(cc=other), k_near)
    give_far = [copy_to(out_half(0), slot(sg, 0, z, 0, both), dev(zz=opp, cc=0), k_far[0]), None]
    take_near = copy_to(out_half(0), slot(sg, 0, z, core, both), dev(cc=other), k_near)
    take_far = copy_to(out_half(0), slot(sg, 0, opp, core, both), dev(zz=opp), k_far[0])
    give_far[1] = pltpu.make_async_remote_copy(
        src_ref=out_half(1), dst_ref=slot(sg, 0, z, 1, both), send_sem=send_sem.at[k_far[1]], recv_sem=recv_sem.at[k_far[0]],
        device_id=dev(zz=opp, cc=1), device_id_type=MESH,
    )

    k_t = [(number(), number()) for _ in range(PARTS)]
    parts = [pl.ds(k * PART, PART) for k in range(PARTS)]

    def tslot(dy, cc, rows=None, cols=slice(None)):
        start, size = (0, 32) if rows is None else rows
        return tg.at[pl.ds(pl.multiple_of(64 * wrap(y + dy) + 32 * cc + start, 16), size), cols]

    def tcopy(device, k, which):
        return pltpu.make_async_remote_copy(
            src_ref=tgt.at[:, parts[k]], dst_ref=tslot(0, core, cols=parts[k]),
            send_sem=send_sem.at[k_t[k][which]], recv_sem=recv_sem.at[k_t[k][0] + core],
            device_id=device, device_id_type=MESH,
        )

    give_t = [tcopy(dev(zz=opp, cc=1), k, 0) for k in range(PARTS)]
    give_t_here = [tcopy(dev(cc=0), k, 1) for k in range(PARTS)]
    take_t = [
        [copy_to(tgt.at[:, parts[k]], tslot(0, cc, cols=parts[k]), dev(zz=opp, cc=1), k_t[k][cc]) for cc in (0, 1)]
        for k in range(PARTS)
    ]

    def targets_out(k):
        give_t[k].start()

        @pl.when(core == 1)
        def _():
            give_t_here[k].start()

    targets_out(0)

    @pl.when(mine)
    def _():
        give_near.start()

    @pl.when(jnp.logical_not(mine))
    def _():
        give_far[0].start()
        give_far[1].start()

    for k in range(1, PARTS):
        targets_out(k)
    small = [
        send(own.at[0], far.at[0], dev(cc=other)),
        send(own.at[1], far.at[1], dev(cc=other)),
        send(own.at[2, :, pl.ds(0, COLS)], far.at[2, :, pl.ds(0, COLS)], dev(zz=opp)),
    ]

    @pl.when(mine)
    def _():
        slot(sg, 0, z, core, both)[...] = out_half(core)[...]

    @pl.when(core == 0)
    def _():
        tslot(0, 0)[...] = tgt[...]

    @pl.when(jnp.logical_not(mine))
    def _():
        take_near.wait_recv()

    gathers = [Gather(sg, n) for n in range(CHUNKS)]
    for g in gathers:
        g.near()

    yc = {}

    def targets_start(k):
        for cc in (0, 1):
            if cc == 0:

                @pl.when(core == 1)
                def _():
                    take_t[k][0].wait_recv()
            else:
                take_t[k][1].wait_recv()
            ref = tslot(0, cc, cols=parts[k])
            for d in (1, -1):
                yc[k, cc, d] = send(ref, ref, dev(dy=d))

    targets_start(0)
    take_far.wait_recv()
    for g in gathers:
        g.far()
    for g in gathers:
        g.far_x()

    def targets_on(k):
        for cc in (0, 1):
            for d in (1, -1):
                yc[k, cc, d].wait_recv()
                ref = tslot(-d, cc, (0 if d == 1 else 16, 16), parts[k])
                yc[k, cc, "f", d] = send(ref, ref, dev(dy=d))

    def targets_in(k):
        for cc in (0, 1):
            for d in (1, -1):
                yc[k, cc, "f", d].wait_recv()
        cols = slice(k * PART, k * PART + PART)
        half_t[:, cols] = 0.5 * jnp.sum(tg[:, cols] * tg[:, cols], axis=0, keepdims=True)
        for b in range(k * PART // 128, (k + 1) * PART // 128):
            here = slice(128 * b, 128 * b + 128)
            high, low = halves(tg[:, here].T * SCALE)
            tcat[here, 0:256] = high
            tcat[here, 256:512] = high
            tcat[here, 512:768] = low
            cb[here, :] = jnp.broadcast_to(half_t[:, here] * SCALE, (128, 128)).T

    gathers[0].near_on()
    for k in range(1, PARTS):
        targets_start(k)
    for g in gathers[1:]:
        g.near_on()
    targets_on(0)
    for g in gathers:
        g.far_on()
    for k in range(1, PARTS):
        targets_on(k)
    gathers[0].last()
    targets_in(0)

    def split_points(buf, n):
        cols = pl.ds(pl.multiple_of(n * WIDTH, WIDTH), WIDTH)
        a = buf[:, cols]
        high, low = halves(a)
        scat[0:256, cols] = high
        scat[256:512, cols] = low
        scat[512:768, cols] = high
        return 0.5 * jnp.sum(a * a, axis=0, keepdims=True)

    def split_chunk(buf, n, norm):
        def step(m, _):
            cols = pl.ds(pl.multiple_of(m * WIDTH, WIDTH), WIDTH)
            norm(cols, split_points(buf, m))
            return 0

        lax.fori_loop(n * CHUNK // WIDTH, (n + 1) * CHUNK // WIDTH, step, 0)

    def blocks(n):
        return [slice(k, k + BLOCK) for k in range(n * CHUNK, (n + 1) * CHUNK, BLOCK)]

    def wide(a, pieces):
        return jnp.concatenate([a] * pieces, axis=1)

    def lane_top(a):
        return functools.reduce(jnp.maximum, [a[:, k : k + 128] for k in range(0, a.shape[1], 128)])

    def row_pass(body, first=0, size=COLS):
        def step(r, acc):
            return acc + body(pl.ds(pl.multiple_of(r * 8, 8), 8))

        acc = lax.fori_loop(first // 8, (first + size) // 8, step, jnp.zeros((8, ROWS), F32), unroll=4)
        return jnp.sum(acc, axis=0, keepdims=True)

    row_lse = []
    for k in range(PARTS):
        here = slice(k * PART, k * PART + PART)
        if k > 0:
            targets_in(k)

        for n, g in enumerate(gathers):
            if k == 0:
                if n > 0:
                    g.last()
                g.finish()

                def norm(cols, value):
                    frow[:, cols] = value

                split_chunk(sg, n, norm)
            for cols in blocks(n):
                cross = jnp.dot(tcat[here, :], scat[:, cols], preferred_element_type=F32)
                q[here, cols] = cross
                phi[:, cols] = jnp.max(cross - wide(cb[here, :], BLOCK // 128), axis=0, keepdims=True)
        top = phi[...]
        row_lse.append(top + jnp.log(row_pass(lambda rows: jnp.exp2(q[rows, :] - wide(cb[rows, :], ROWS // 128) - top), k * PART, PART)) * LOG2E)

    arrived(small)
    slw[...] = jnp.where(mine, own[0], far[0])
    tim[...] = jnp.where(mine, own[1], far[1])
    tlw[...] = jnp.where(core == 0, own[2], far[2])[:, 0:COLS]

    for k in range(PARTS):
        give_t[k].wait_send()

    @pl.when(core == 1)
    def _():
        for k in range(PARTS):
            give_t_here[k].wait_send()

    @pl.when(mine)
    def _():
        give_near.wait_send()

    @pl.when(jnp.logical_not(mine))
    def _():
        give_far[0].wait_send()
        give_far[1].wait_send()

    copies = to_group(vr.at[0], lse_over_first(jnp.stack(row_lse)))
    arrived(copies)
    lse = lse_over_first(vr[0])
    phi[...] = slw[...] * LOG2E - lse
    frow[...] = frow[...] + EPSILON * (slw[...] - LN2 * lse)

    def join_tops():
        for b in range(0, COLS, 128):
            nb[b : b + 128, :] = jnp.broadcast_to(jnp.max(nb[b : b + 128, :], axis=1, keepdims=True), (128, 128))

    def top_step(r, _):
        rows = pl.ds(pl.multiple_of(r * 8, 8), 8)
        nb[rows, :] = lane_top(q[rows, :] + phi[...])
        return 0

    def exp_step(r, _):
        rows = pl.ds(pl.multiple_of(r * 8, 8), 8)
        p = jnp.exp2(q[rows, :] + phi[...] - wide(nb[rows, :], ROWS // 128))
        e[rows, :] = p
        sb[rows, :] = tiles(p)
        return 0

    def column_lse():
        return column_top(nb), column_sum(sb)

    lax.fori_loop(0, COLS // 8, top_step, 0, unroll=4)
    join_tops()
    lax.fori_loop(0, COLS // 8, exp_step, 0, unroll=4)
    ntop, total = column_lse()
    copies = to_line(vc.at[0], ntop + jnp.log(total) * LOG2E)

    def split_step(r, _):
        rows = pl.ds(pl.multiple_of(r * 16, 16), 16)
        high, low = halves(e[rows, :])
        eh[rows, :] = high
        el[rows, :] = low
        return 0

    lax.fori_loop(0, COLS // 16, split_step, 0, unroll=2)
    arrived(copies)
    factor = jnp.exp2(ntop + (tlw[...] * LOG2E - lse_over_first(vc[0])))
    as_column(factor, cb)

    def against_column(rows):
        return e[rows, :] * wide(cb[rows, :], ROWS // 128)

    copies = to_group(vr.at[1], row_pass(against_column))
    arrived(copies)
    total = jnp.sum(vr[1], axis=0)
    f2[...] = frow[...] + EPSILON * (slw[...] - jnp.log(total))
    phi[...] = jnp.exp(slw[...]) / total
    potential = send(f2, ff, dev(zz=opp))

    def weigh_step(r, _):
        rows = pl.ds(pl.multiple_of(r * 8, 8), 8)
        sb[rows, :] = tiles(e[rows, :] * phi[...])
        return 0

    lax.fori_loop(0, COLS // 8, weigh_step, 0, unroll=4)
    copies = to_line(vc.at[1], factor * column_sum(sb))
    arrived(copies)
    dual = factor * (jnp.exp(tlw[...]) / jnp.sum(vc[1], axis=0))
    as_column(dual, cb)

    potential.wait_recv()

    copies = to_group(vr.at[2], row_pass(against_column))
    high, low = halves(tg[...] * dual)
    tw[0:256, :] = high
    tw[256:512, :] = low
    def wz(zz, cols, dx=None):
        return w.at[slice(None) if dx is None else wrap(x + dx), zz, core, :, cols]

    c = {}

    def weigh(m):
        cols = slice(m * BLOCK, m * BLOCK + BLOCK)
        acc = jnp.dot(tw[0:256, :], eh[:, cols], preferred_element_type=F32)
        acc = acc + jnp.dot(tw[0:256, :], el[:, cols], preferred_element_type=F32)
        acc = acc + jnp.dot(tw[256:512, :], eh[:, cols], preferred_element_type=F32)
        w[:, :, :, :, cols] = acc.reshape(SIDE, SIDE, 2, 8, BLOCK)
        n = m * BLOCK // CHUNK
        if (m + 1) * BLOCK == (n + 1) * CHUNK:
            cols = chunk_cols(n)
            c[n, "core"] = send(w.at[:, :, other, :, cols], r0.at[:, :, :, cols], dev(cc=other))

    def rx_start(n, key, zz, k):
        for d in (1, -1):
            cut = chunk_half(n, d)
            c[n, key, d] = send(wz(zz, cut, 2), rx1.at[k, :, cut], dev(d))

    def rx_middle(n, key, zz, k):
        for d in (1, -1):
            cut = chunk_half(n, d)
            c[n, key, d].wait_recv()
            ref = wz(zz, cut, d)
            ref[...] = ref[...] + rx1[k, :, cut]
            c[n, key, "s", d] = send(wz(zz, chunk_cols(n), d), rx2.at[k, 0 if d == 1 else 1, :, chunk_cols(n)], dev(d))

    def rx_end(n, key, zz, k):
        for d in (1, -1):
            c[n, key, "s", d].wait_recv()
        cols = chunk_cols(n)
        return wz(zz, cols, 0)[...] + rx2[k, 0, :, cols] + rx2[k, 1, :, cols]

    def rx_direct(n, key, zz, k):
        for i, d in enumerate((2, 1, -1)):
            c[n, key, d] = send(wz(zz, chunk_cols(n), d), rd.at[k, i, :, chunk_cols(n)], dev(d))

    def rx_sum(n, key, zz, k):
        cols = chunk_cols(n)
        for d in (1, -1, 2):
            c[n, key, d].wait_recv()
        return wz(zz, cols, 0)[...] + rd[k, 0, :, cols] + rd[k, 1, :, cols] + rd[k, 2, :, cols]

    def rs1(n):
        cols = chunk_cols(n)
        c[n, "core"].wait_recv()
        ref = w.at[:, :, core, :, cols]
        ref[...] = ref[...] + r0[:, :, :, cols]
        c[n, "mate"] = send(wz(mate, cols), rb.at[:, :, cols], dev(zz=mate))
        rx_direct(n, "m", mates_opp, 0)
        rx_start(n, "o", opp, 0)

    def rs2(n):
        cols = chunk_cols(n)
        c[n, "mate"].wait_recv()
        ref = wz(z, cols)
        ref[...] = ref[...] + rb[:, :, cols]
        rx_direct(n, "z", z, 1)
        rx_middle(n, "o", opp, 0)

    def rs3(n):
        cols = chunk_cols(n)
        qs = wz(mates_opp, cols, 0)
        qs[...] = rx_sum(n, "m", mates_opp, 0)
        c[n, "last"] = send(qs, qb.at[:, cols], dev(zz=mate))

    def point_rows(zz):
        return pl.ds(pl.multiple_of((x * SIDE + zz) * 16 + 8 * core, 8), 8)

    mgathers = [Gather(mg, n) for n in range(CHUNKS)]
    k_out = [(number(), number()) for _ in range(CHUNKS)]
    outs = []

    def rs4(n):
        cols = chunk_cols(n)
        g = mgathers[n]
        ratio = tim[:, cols] / jnp.sum(vr[2, :, :, cols], axis=0)
        keep = 1.0 - tim[:, cols]
        share = rx_sum(n, "z", z, 1)
        mg[point_rows(z), cols] = keep * sg[point_rows(z), cols] + ratio * share
        g.near()
        share = rx_end(n, "o", opp, 0)
        c[n, "last"].wait_recv()
        mg[point_rows(opp), cols] = keep * sg[point_rows(opp), cols] + ratio * (share + qb[:, cols])
        g.far()
        g.far_x()
        here = mv.at[pl.ds(pl.multiple_of(8 * core, 8), 8), cols]
        there = mv.at[pl.ds(pl.multiple_of(8 * other, 8), 8), cols]

        def result(zz, device, k):
            return pltpu.make_async_remote_copy(
                src_ref=slot(mg, 0, zz, core, cols), dst_ref=here, send_sem=send_sem.at[k], recv_sem=recv_sem.at[k_out[n][0] + core],
                device_id=device, device_id_type=MESH,
            )

        far_out = result(opp, dev(zz=opp, cc=block), k_out[n][0])
        near_out = result(z, dev(cc=other), k_out[n][1])
        far_out.start()
        started.append(far_out)

        @pl.when(mine)
        def _():
            here[...] = mg[point_rows(z), cols]

        @pl.when(jnp.logical_not(mine))
        def _():
            near_out.start()

        def result_in(ref, k):
            return pltpu.make_async_remote_copy(
                src_ref=ref, dst_ref=ref, send_sem=send_sem.at[k_out[n][0]], recv_sem=recv_sem.at[k],
                device_id=dev(cc=other), device_id_type=MESH,
            )

        outs.append((near_out, result_in(here, k_out[n][0] + core), result_in(there, k_out[n][0] + other)))

    half = ROWS // BLOCK // 2
    for m in range(half):
        weigh(m)
    weigh(half)
    rs1(0)
    for m in range(half + 1, 2 * half):
        weigh(m)
    rs2(0)
    rs1(1)
    rs3(0)
    rs2(1)
    arrived(copies)
    rs4(0)
    rs3(1)
    mgathers[0].near_on()
    rs4(1)
    mgathers[0].far_on()
    mgathers[1].near_on()
    mgathers[0].last()
    mgathers[1].far_on()

    def last_chunk(n):
        def norm(cols, value):
            phi[:, cols] = (f2[:, cols] - value) * SCALE

        split_chunk(mg, n, norm)
        for k, cols in enumerate(blocks(n)):
            scores = jnp.dot(tcat[...], scat[:, cols], preferred_element_type=F32) + phi[:, cols]
            q[:, cols] = scores
            nb[...] = lane_top(scores) if k == 0 else jnp.maximum(nb[...], lane_top(scores))

    def last_sums(n):
        join_tops()

        def step(r, _):
            rows = pl.ds(pl.multiple_of(r * 8, 8), 8)
            sb[rows, :] = tiles(jnp.exp2(q[rows, chunk_cols(n)] - wide(nb[rows, :], CHUNK // 128)))
            return 0

        lax.fori_loop(0, COLS // 8, step, 0, unroll=8)
        ntop, total = column_lse()
        return ntop + jnp.log(total) * LOG2E

    def results():
        for near_out, half_here, half_there in outs:
            half_there.wait_recv()

            @pl.when(jnp.logical_not(mine))
            def _():
                half_here.wait_recv()
                near_out.wait_send()

        fr[...] = jnp.where(mine, f2[...], ff[...])
        for store in stores[:2]:
            store.start()

    col_lse = []
    for n, g in enumerate(mgathers):
        g.finish()
        last_chunk(n)
        if n == 0:
            results()
        if n < CHUNKS - 1:
            mgathers[n + 1].last()
        col_lse.append(last_sums(n))
    home = z + core * (opp - z)
    part[...] = lse_over_first(jnp.stack(col_lse)) - half_t[...] * SCALE

    def to_owner(dy, cc, k, base):
        return pltpu.make_async_remote_copy(
            src_ref=part, dst_ref=vc.at[2, line_slot], send_sem=send_sem.at[k], recv_sem=recv_sem.at[base + core],
            device_id=dev(dy=dy, zz=home, cc=cc), device_id_type=MESH,
        )

    def from_owner(k):
        return copy_to(part, vc.at[2, line_slot], dev(cc=other), k)

    waits = []
    for dy in (2, 1, -1):
        base, more = number(), number()
        for cc, k in ((0, base), (1, more)):
            copy = to_owner(dy, cc, k, base)
            copy.start()
            started.append(copy)
        waits += [from_owner(base), from_owner(more)]
    base, more = number(), number()
    to_one, to_zero = to_owner(0, 1, more, base), to_owner(0, 0, base, base)
    to_one.start()
    started.append(to_one)

    @pl.when(core == 1)
    def _():
        to_zero.start()
        from_owner(base).wait_recv()

    @pl.when(core == 0)
    def _():
        vc[2, line_slot] = part[...]

    from_owner(more).wait_recv()
    arrived(waits)
    fc[...] = EPSILON * (own[2][:, 0:COLS] - LN2 * lse_over_first(vc[2]))
    stores[2].start()
    for store in stores:
        store.wait()

    @pl.when(core == 1)
    def _():
        to_zero.wait_send()

    for copy in started:
        copy.wait_send()


def per_device(sources, targets, source_logw, target_logw, times):
    anywhere = pl.BlockSpec(memory_space=pl.ANY)
    rowp, moved, colp = pl.pallas_call(
        kernel,
        out_shape=(
            jax.ShapeDtypeStruct((1, ROWS), F32),
            jax.ShapeDtypeStruct((16, ROWS), F32),
            jax.ShapeDtypeStruct((1, COLS), F32),
        ),
        in_specs=[anywhere] * 5,
        out_specs=(anywhere,) * 3,
        scratch_shapes=[
            pltpu.VMEM((16, ROWS), F32),
            pltpu.VMEM((32, COLS), F32),
            pltpu.VMEM((3, 1, ROWS), F32),
            pltpu.VMEM((3, 1, ROWS), F32),
            pltpu.VMEM((1, ROWS), F32),
            pltpu.VMEM((1, COLS), F32),
            pltpu.VMEM((1, ROWS), F32),
            pltpu.VMEM((FEATURES, ROWS), F32),
            pltpu.VMEM((FEATURES, COLS), F32),
            pltpu.VMEM((FEATURES, ROWS), F32),
            pltpu.VMEM((16, ROWS), F32),
            pltpu.VMEM((COLS, 3 * FEATURES), BF16),
            pltpu.VMEM((3 * FEATURES, ROWS), BF16),
            pltpu.VMEM((COLS, ROWS), F32),
            pltpu.VMEM((COLS, ROWS), F32),
            pltpu.VMEM((SIDE, SIDE, 2, 8, ROWS), F32),
            pltpu.VMEM((2 * FEATURES, COLS), BF16),
            pltpu.VMEM((COLS, ROWS), BF16),
            pltpu.VMEM((COLS, ROWS), BF16),
            pltpu.VMEM((SIDE, SIDE, 8, ROWS), F32),
            pltpu.VMEM((SIDE, 8, ROWS), F32),
            pltpu.VMEM((1, 8, ROWS), F32),
            pltpu.VMEM((1, 2, 8, ROWS), F32),
            pltpu.VMEM((2, 3, 8, ROWS), F32),
            pltpu.VMEM((8, ROWS), F32),
            pltpu.VMEM((3, GROUP, 1, ROWS), F32),
            pltpu.VMEM((3, LINE, 1, COLS), F32),
            pltpu.VMEM((COLS, 128), F32),
            pltpu.VMEM((COLS, 128), F32),
            pltpu.VMEM((COLS, 128), F32),
            pltpu.VMEM((1, COLS), F32),
            pltpu.VMEM((1, ROWS), F32),
            pltpu.VMEM((1, ROWS), F32),
            pltpu.VMEM((1, ROWS), F32),
            pltpu.VMEM((1, ROWS), F32),
            pltpu.VMEM((1, ROWS), F32),
            pltpu.VMEM((1, COLS), F32),
            pltpu.VMEM((1, COLS), F32),
            pltpu.SemaphoreType.DMA((COPIES,)),
            pltpu.SemaphoreType.DMA((COPIES,)),
            pltpu.SemaphoreType.DMA((5,)),
        ],
        compiler_params=pltpu.CompilerParams(
            collective_id=0, has_side_effects=True, vmem_limit_bytes=60 * 1024 * 1024
        ),
    )(sources, targets, source_logw[None], target_logw[None], times[None])
    return rowp[0], moved, colp[0]


def solution(mesh):
    return jax.shard_map(
        per_device,
        mesh=mesh,
        in_specs=(P("tgt", "src"), P("src", "tgt"), P("src"), P("tgt"), P("src")),
        out_specs=(P("src"), P("tgt", "src"), P("tgt")),
        check_vma=False,
    )
```

```python
import functools

import jax
import jax.numpy as jnp
from jax import lax
from jax.experimental import pallas as pl
from jax.experimental.pallas import tpu as pltpu
from jax.sharding import PartitionSpec as P

MESH = pl.DeviceIdType.MESH
F32 = jnp.float32
BF16 = jnp.bfloat16
EPSILON = 16.0
LOG2E = 1.4426950408889634
LN2 = 0.6931471805599453
SCALE = LOG2E / EPSILON

FEATURES = 256
ROWS = 2048
COLS = 1024
SIDE = 4
GROUP = 16
LINE = 8
ARRIVALS = 179
DEPARTURES = 44
CHUNKS = 2
CHUNK = ROWS // CHUNKS
PIECES = 4
PIECE = ROWS // PIECES
WIDTH = 256
PARTS = 2
PART = COLS // PARTS
BLOCK = 512


def halves(a):
    high = a.astype(BF16)
    return high, (a - high.astype(F32)).astype(BF16)


def tiles(a):
    return functools.reduce(lambda p, r: p + r, [a[:, 128 * k : 128 * k + 128] for k in range(a.shape[1] // 128)])


def kernel(
    src_h, tgt_h, slw_h, tlw_h, tim_h,
    rowp, moved, colp,
    src, tgt, own, far, slw, tlw, tim, sg, tg, mg, mv, tcat, scat, q, e, w, tw, eh, el,
    r0, rb, rx1, rx2, rd, qb, vr, vc, nb, sb, cb, part, frow, phi, f2, ff, fr, fc, half_t,
    send_sem, recv_sem, in_sem,
):
    me_s, me_t = lax.axis_index("src"), lax.axis_index("tgt")
    x, z = me_t // SIDE, me_t % SIDE
    y, core = me_s // 2, me_s % 2
    block = z // 2
    mate = z + 1 - 2 * (z % 2)
    opp = SIDE - 1 - z
    mates_opp = SIDE - 1 - mate
    other = 1 - core
    mine = core == block
    started = []

    def wrap(value):
        return lax.rem(value + SIDE, SIDE)

    def dev(dx=0, dy=0, zz=z, cc=core):
        return (wrap(y + dy) * 2 + cc, wrap(x + dx) * SIDE + zz)

    def copy_to(source, target, device, k, out=0):
        return pltpu.make_async_remote_copy(
            src_ref=source, dst_ref=target, send_sem=send_sem.at[out], recv_sem=recv_sem.at[k],
            device_id=device, device_id_type=MESH,
        )

    count, leaves = [0], [0]

    def number():
        count[0] += 1
        return count[0] - 1

    def leave():
        leaves[0] += 1
        return leaves[0] - 1

    def send(source, target, device, out=None, k=None):
        copy = copy_to(source, target, device, number() if k is None else k, leave() if out is None else out)
        copy.start()
        if out is None:
            started.append(copy)
        return copy

    def all_left(ref, out):
        started.append(copy_to(ref, ref, dev(cc=other), 0, out))

    loads = [
        pltpu.make_async_copy(a, b, in_sem.at[k])
        for k, (a, b) in enumerate(((src_h, src), (tgt_h, tgt), (slw_h, own.at[0]), (tim_h, own.at[1]), (tlw_h, own.at[2, :, pl.ds(0, COLS)])))
    ]
    for load in loads:
        load.start()
    stores = [pltpu.make_async_copy(a, b, in_sem.at[k]) for k, (a, b) in enumerate(((mv, moved), (fr, rowp), (fc, colp)))]
    barrier = pltpu.get_barrier_semaphore()
    near = [dev(1), dev(-1), dev(2), dev(dy=1), dev(dy=-1), dev(zz=mate), dev(zz=opp), dev(zz=opp, cc=other), dev(cc=other)]
    for device in near:
        pl.semaphore_signal(barrier, inc=1, device_id=device, device_id_type=MESH)
    for load in loads:
        load.wait()
    pl.semaphore_wait(barrier, len(near))

    def slot(buf, dx, zz, cc, cols):
        return buf.at[pl.ds(pl.multiple_of((wrap(x + dx) * SIDE + zz) * 16 + 8 * cc, 8), 8), cols]

    def chunk_cols(n, size=PIECE):
        return pl.ds(n * size, size)

    def chunk_half(n, d, size=PIECE):
        return pl.ds(n * size + (0 if d == 1 else size // 2), size // 2)

    class Gather:
        def __init__(self, buf, n, size):
            self.buf, self.n, self.size = buf, n, size
            self.cols = chunk_cols(n, size)
            self.c = {}
            self.out, self.shared = leave(), number()
            all_left(buf.at[0:240, self.cols], self.out)

        def share(self, dx, zz):
            ref = slot(self.buf, dx, zz, core, self.cols)
            send(ref, ref, dev(cc=other), self.out, self.shared)

        def to_mate(self, key, dx, zz):
            ref = slot(self.buf, dx, zz, core, self.cols)
            self.c[key] = send(ref, ref, dev(zz=mate), self.out)

        def round_x(self, key, zz, shifts):
            ref = slot(self.buf, 0, zz, core, self.cols)
            for d in shifts:
                self.c[key, d] = send(ref, ref, dev(d), self.out)

        def near(self):
            self.round_x("n", z, (2, 1, -1))
            self.to_mate(("m", 0), 0, z)
            self.share(0, z)

        def far(self, pass_on=True):
            if pass_on:
                self.to_mate("fm", 0, opp)
            self.share(0, opp)

        def far_x(self):
            self.round_x("f", opp, (1, -1))

        def near_on(self):
            for d in (1, -1, 2):
                self.c["n", d].wait_recv()
                self.to_mate(("m", -d), -d, z)
                self.share(-d, z)

        def far_mate(self):
            if "fm" in self.c:
                self.c["fm"].wait_recv()
            self.round_x("g", mates_opp, (2, 1, -1))
            self.share(0, mates_opp)

        def far_on(self):
            for d in (1, -1):
                self.c["f", d].wait_recv()
                ref = slot(self.buf, -d, opp, core, chunk_half(self.n, d, self.size))
                self.c["ff", d] = send(ref, ref, dev(d), self.out)
                self.share(-d, opp)

        def last(self):
            self.c["m", 0].wait_recv()
            self.share(0, mate)
            for d in (1, -1):
                self.c["ff", d].wait_recv()
            self.share(2, opp)
            for d in (1, -1, 2):
                self.c["m", -d].wait_recv()
                self.share(-d, mate)
                self.c["g", d].wait_recv()
                self.share(-d, mates_opp)

        def finish(self):
            ref = self.buf.at[0:128, self.cols]
            copy_to(ref, ref, dev(cc=other), self.shared).wait_recv()

    def group_devices():
        return [
            dev(dx, zz=zz, cc=cc)
            for dx in (2, 1, -1, 0)
            for zz in (mate, z)
            for cc in (other, core)
            if not (dx == 0 and zz is z and cc is core)
        ]

    group_slot = x * 4 + (z % 2) * 2 + core
    line_slot = y * 2 + block

    def to_all(buf, k, row, devices):
        buf[k] = row
        out, arrival = leave(), number()
        for device in devices:
            send(buf.at[k], buf.at[k], device, out, arrival)
        whole = buf.at[0 : len(devices)]
        all_left(whole, out)
        return [copy_to(whole, whole, dev(cc=other), arrival)]

    def to_group(buf, row):
        return to_all(buf, group_slot, row, group_devices())

    line = [(dy, zz, cc) for dy in (2, 1, -1, 0) for zz, cc in ((opp, other), (z, core)) if not (dy == 0 and zz is z)]

    def to_line(buf, row):
        return to_all(buf, line_slot, row, [dev(dy=dy, zz=zz, cc=cc) for dy, zz, cc in line])

    def arrived(copies):
        for copy in copies:
            copy.wait_recv()

    def lse_over_first(a):
        top = jnp.max(a, axis=0)
        return top + jnp.log(jnp.sum(jnp.exp2(a - top[None]), axis=0)) * LOG2E

    def as_column(row, ref):
        for b in range(COLS // 128):
            piece = row[:, 128 * b : 128 * b + 128]
            ref[128 * b : 128 * b + 128, :] = jnp.broadcast_to(piece, (128, 128)).T

    def column_top(ref):
        return jnp.concatenate([ref[128 * b : 128 * b + 128, :].T[0:1, :] for b in range(COLS // 128)], axis=1)

    def column_sum(ref):
        return jnp.concatenate(
            [jnp.sum(ref[128 * b : 128 * b + 128, :].T, axis=0, keepdims=True) for b in range(COLS // 128)], axis=1
        )

    both = pl.ds(0, ROWS)
    k_near, s_near = number(), leave()
    k_far, s_far = number(), (leave(), leave())

    def out_half(cc):
        return src.at[pl.ds(pl.multiple_of(8 * cc, 8), 8), :]

    give_near = copy_to(out_half(other), slot(sg, 0, z, other, both), dev(cc=other), k_near, s_near)
    give_far = [copy_to(out_half(cc), slot(sg, 0, z, cc, both), dev(zz=opp, cc=cc), k_far, s_far[cc]) for cc in (0, 1)]
    take_near = copy_to(out_half(0), slot(sg, 0, z, core, both), dev(cc=other), k_near)
    take_far = copy_to(out_half(0), slot(sg, 0, opp, core, both), dev(zz=opp), k_far)

    k_t = [(number(), number()) for _ in range(PARTS)]
    s_t = [(leave(), leave()) for _ in range(PARTS)]
    parts = [pl.ds(k * PART, PART) for k in range(PARTS)]

    def tslot(dy, cc, rows=None, cols=slice(None)):
        start, size = (0, 32) if rows is None else rows
        return tg.at[pl.ds(pl.multiple_of(64 * wrap(y + dy) + 32 * cc + start, 16), size), cols]

    def tcopy(device, k, which):
        return pltpu.make_async_remote_copy(
            src_ref=tgt.at[:, parts[k]], dst_ref=tslot(0, core, cols=parts[k]),
            send_sem=send_sem.at[s_t[k][which]], recv_sem=recv_sem.at[k_t[k][0] + core],
            device_id=device, device_id_type=MESH,
        )

    give_t = [tcopy(dev(zz=opp, cc=1), k, 0) for k in range(PARTS)]
    give_t_here = [tcopy(dev(cc=0), k, 1) for k in range(PARTS)]
    take_t = [
        [copy_to(tgt.at[:, parts[k]], tslot(0, cc, cols=parts[k]), dev(zz=opp, cc=1), k_t[k][cc]) for cc in (0, 1)]
        for k in range(PARTS)
    ]

    def targets_out(k):
        give_t[k].start()

        @pl.when(core == 1)
        def _():
            give_t_here[k].start()

    targets_out(0)

    @pl.when(mine)
    def _():
        give_near.start()

    @pl.when(jnp.logical_not(mine))
    def _():
        give_far[0].start()
        give_far[1].start()

    for k in range(1, PARTS):
        targets_out(k)
    small = [
        send(own.at[0], far.at[0], dev(cc=other)),
        send(own.at[1], far.at[1], dev(cc=other)),
        send(own.at[2, :, pl.ds(0, COLS)], far.at[2, :, pl.ds(0, COLS)], dev(zz=opp)),
    ]

    @pl.when(mine)
    def _():
        slot(sg, 0, z, core, both)[...] = out_half(core)[...]

    @pl.when(core == 0)
    def _():
        tslot(0, 0)[...] = tgt[...]

    @pl.when(jnp.logical_not(mine))
    def _():
        take_near.wait_recv()

    gathers = [Gather(sg, n, CHUNK) for n in range(CHUNKS)]
    for g in gathers:
        g.near()

    yc = {}
    s_y = [leave() for _ in range(PARTS)]
    for k in range(PARTS):
        all_left(tg.at[0:192, parts[k]], s_y[k])

    def targets_start(k):
        for cc in (0, 1):
            if cc == 0:

                @pl.when(core == 1)
                def _():
                    take_t[k][0].wait_recv()
            else:
                take_t[k][1].wait_recv()
            ref = tslot(0, cc, cols=parts[k])
            for d in (1, -1):
                yc[k, cc, d] = send(ref, ref, dev(dy=d), s_y[k])

    targets_start(0)
    take_far.wait_recv()
    for g in gathers:
        g.far()
    for g in gathers:
        g.far_x()

    def targets_on(k):
        for cc in (0, 1):
            for d in (1, -1):
                yc[k, cc, d].wait_recv()
                ref = tslot(-d, cc, (0 if d == 1 else 16, 16), parts[k])
                yc[k, cc, "f", d] = send(ref, ref, dev(dy=d), s_y[k])

    def targets_in(k):
        for cc in (0, 1):
            for d in (1, -1):
                yc[k, cc, "f", d].wait_recv()
        cols = slice(k * PART, k * PART + PART)
        half_t[:, cols] = 0.5 * jnp.sum(tg[:, cols] * tg[:, cols], axis=0, keepdims=True)
        for b in range(k * PART // 128, (k + 1) * PART // 128):
            here = slice(128 * b, 128 * b + 128)
            high, low = halves(tg[:, here].T * SCALE)
            tcat[here, 0:256] = high
            tcat[here, 256:512] = high
            tcat[here, 512:768] = low
            cb[here, :] = jnp.broadcast_to(half_t[:, here] * SCALE, (128, 128)).T

    gathers[0].near_on()
    for k in range(1, PARTS):
        targets_start(k)
    for g in gathers[1:]:
        g.near_on()
    targets_on(0)
    for g in gathers:
        g.far_mate()
        g.far_on()
    for k in range(1, PARTS):
        targets_on(k)
    gathers[0].last()
    targets_in(0)

    def split_points(buf, n):
        cols = pl.ds(pl.multiple_of(n * WIDTH, WIDTH), WIDTH)
        a = buf[:, cols]
        high, low = halves(a)
        scat[0:256, cols] = high
        scat[256:512, cols] = low
        scat[512:768, cols] = high
        return 0.5 * jnp.sum(a * a, axis=0, keepdims=True)

    def split_chunk(buf, n, size, norm):
        def step(m, _):
            cols = pl.ds(pl.multiple_of(m * WIDTH, WIDTH), WIDTH)
            norm(cols, split_points(buf, m))
            return 0

        lax.fori_loop(n * size // WIDTH, (n + 1) * size // WIDTH, step, 0)

    def blocks(n, size):
        return [slice(k, k + BLOCK) for k in range(n * size, (n + 1) * size, BLOCK)]

    def wide(a, pieces):
        return jnp.concatenate([a] * pieces, axis=1)

    def lane_top(a):
        return functools.reduce(jnp.maximum, [a[:, k : k + 128] for k in range(0, a.shape[1], 128)])

    def row_pass(body, first=0, size=COLS):
        def step(r, acc):
            return acc + body(pl.ds(pl.multiple_of(r * 8, 8), 8))

        acc = lax.fori_loop(first // 8, (first + size) // 8, step, jnp.zeros((8, ROWS), F32), unroll=4)
        return jnp.sum(acc, axis=0, keepdims=True)

    row_lse = []
    for k in range(PARTS):
        here = slice(k * PART, k * PART + PART)
        if k > 0:
            targets_in(k)

        for n, g in enumerate(gathers):
            if k == 0:
                if n > 0:
                    g.last()
                g.finish()

                def norm(cols, value):
                    frow[:, cols] = value

                split_chunk(sg, n, CHUNK, norm)
            for cols in blocks(n, CHUNK):
                cross = jnp.dot(tcat[here, :], scat[:, cols], preferred_element_type=F32)
                q[here, cols] = cross
                phi[:, cols] = jnp.max(cross - wide(cb[here, :], BLOCK // 128), axis=0, keepdims=True)
        top = phi[...]
        row_lse.append(top + jnp.log(row_pass(lambda rows: jnp.exp2(q[rows, :] - wide(cb[rows, :], ROWS // 128) - top), k * PART, PART)) * LOG2E)

    arrived(small)
    slw[...] = jnp.where(mine, own[0], far[0])
    tim[...] = jnp.where(mine, own[1], far[1])
    tlw[...] = jnp.where(core == 0, own[2], far[2])[:, 0:COLS]

    for k in range(PARTS):
        give_t[k].wait_send()

    @pl.when(core == 1)
    def _():
        for k in range(PARTS):
            give_t_here[k].wait_send()

    @pl.when(mine)
    def _():
        give_near.wait_send()

    @pl.when(jnp.logical_not(mine))
    def _():
        give_far[0].wait_send()
        give_far[1].wait_send()

    copies = to_group(vr.at[0], lse_over_first(jnp.stack(row_lse)))
    arrived(copies)
    lse = lse_over_first(vr[0])
    phi[...] = slw[...] * LOG2E - lse
    frow[...] = frow[...] + EPSILON * (slw[...] - LN2 * lse)

    def join_tops():
        for b in range(0, COLS, 128):
            nb[b : b + 128, :] = jnp.broadcast_to(jnp.max(nb[b : b + 128, :], axis=1, keepdims=True), (128, 128))

    def top_step(r, _):
        rows = pl.ds(pl.multiple_of(r * 8, 8), 8)
        nb[rows, :] = lane_top(q[rows, :] + phi[...])
        return 0

    def exp_step(r, _):
        rows = pl.ds(pl.multiple_of(r * 8, 8), 8)
        p = jnp.exp2(q[rows, :] + phi[...] - wide(nb[rows, :], ROWS // 128))
        e[rows, :] = p
        sb[rows, :] = tiles(p)
        return 0

    def column_lse():
        return column_top(nb), column_sum(sb)

    lax.fori_loop(0, COLS // 8, top_step, 0, unroll=4)
    join_tops()
    lax.fori_loop(0, COLS // 8, exp_step, 0, unroll=4)
    ntop, total = column_lse()
    copies = to_line(vc.at[0], ntop + jnp.log(total) * LOG2E)

    def split_step(r, _):
        rows = pl.ds(pl.multiple_of(r * 16, 16), 16)
        high, low = halves(e[rows, :])
        eh[rows, :] = high
        el[rows, :] = low
        return 0

    lax.fori_loop(0, COLS // 16, split_step, 0, unroll=2)
    arrived(copies)
    factor = jnp.exp2(ntop + (tlw[...] * LOG2E - lse_over_first(vc[0])))
    as_column(factor, cb)

    def against_column(rows):
        return e[rows, :] * wide(cb[rows, :], ROWS // 128)

    copies = to_group(vr.at[1], row_pass(against_column))
    arrived(copies)
    total = jnp.sum(vr[1], axis=0)
    f2[...] = frow[...] + EPSILON * (slw[...] - jnp.log(total))
    phi[...] = jnp.exp(slw[...]) / total
    potential = send(f2, ff, dev(zz=opp))

    def weigh_step(r, _):
        rows = pl.ds(pl.multiple_of(r * 8, 8), 8)
        sb[rows, :] = tiles(e[rows, :] * phi[...])
        return 0

    lax.fori_loop(0, COLS // 8, weigh_step, 0, unroll=4)
    copies = to_line(vc.at[1], factor * column_sum(sb))
    arrived(copies)
    dual = factor * (jnp.exp(tlw[...]) / jnp.sum(vc[1], axis=0))
    as_column(dual, cb)

    potential.wait_recv()

    copies = to_group(vr.at[2], row_pass(against_column))
    high, low = halves(tg[...] * dual)
    tw[0:256, :] = high
    tw[256:512, :] = low
    def wz(zz, cols, dx=None):
        return w.at[slice(None) if dx is None else wrap(x + dx), zz, core, :, cols]

    c = {}

    s_w = [leave() for _ in range(PIECES)]
    for n in range(PIECES):
        all_left(mg.at[0:240, chunk_cols(n)], s_w[n])

    def weigh(m):
        cols = slice(m * PIECE, m * PIECE + PIECE)
        acc = jnp.dot(tw[0:256, :], eh[:, cols], preferred_element_type=F32)
        acc = acc + jnp.dot(tw[0:256, :], el[:, cols], preferred_element_type=F32)
        acc = acc + jnp.dot(tw[256:512, :], eh[:, cols], preferred_element_type=F32)
        w[:, :, :, :, cols] = acc.reshape(SIDE, SIDE, 2, 8, PIECE)
        c[m, "core"] = send(w.at[:, :, other, :, cols], r0.at[:, :, :, cols], dev(cc=other), s_w[m])

    def rx_start(n, key, zz, k):
        for d in (1, -1):
            cut = chunk_half(n, d)
            c[n, key, d] = send(wz(zz, cut, 2), rx1.at[k, :, cut], dev(d), s_w[n])

    def rx_middle(n, key, zz, k):
        for d in (1, -1):
            cut = chunk_half(n, d)
            c[n, key, d].wait_recv()
            ref = wz(zz, cut, d)
            ref[...] = ref[...] + rx1[k, :, cut]
            c[n, key, "s", d] = send(wz(zz, chunk_cols(n), d), rx2.at[k, 0 if d == 1 else 1, :, chunk_cols(n)], dev(d), s_w[n])

    def rx_end(n, key, zz, k):
        for d in (1, -1):
            c[n, key, "s", d].wait_recv()
        cols = chunk_cols(n)
        return wz(zz, cols, 0)[...] + rx2[k, 0, :, cols] + rx2[k, 1, :, cols]

    def rx_direct(n, key, zz, k):
        c[n, key] = number()
        for i, d in enumerate((2, 1, -1)):
            send(wz(zz, chunk_cols(n), d), rd.at[k, i, :, chunk_cols(n)], dev(d), s_w[n], c[n, key])

    def rx_sum(n, key, zz, k):
        cols = chunk_cols(n)
        ref = rd.at[k, :, :, cols]
        copy_to(ref, ref, dev(1), c[n, key]).wait_recv()
        return wz(zz, cols, 0)[...] + rd[k, 0, :, cols] + rd[k, 1, :, cols] + rd[k, 2, :, cols]

    def rs1(n):
        cols = chunk_cols(n)
        c[n, "core"].wait_recv()
        ref = w.at[:, :, core, :, cols]
        ref[...] = ref[...] + r0[:, :, :, cols]
        c[n, "mate"] = send(wz(mate, cols), rb.at[:, :, cols], dev(zz=mate), s_w[n])
        rx_direct(n, "m", mates_opp, 0)
        rx_start(n, "o", opp, 0)

    def rs2(n):
        cols = chunk_cols(n)
        c[n, "mate"].wait_recv()
        ref = wz(z, cols)
        ref[...] = ref[...] + rb[:, :, cols]
        rx_direct(n, "z", z, 1)
        rx_middle(n, "o", opp, 0)

    def rs3(n):
        cols = chunk_cols(n)
        qs = wz(mates_opp, cols, 0)
        qs[...] = rx_sum(n, "m", mates_opp, 0)
        c[n, "last"] = send(qs, qb.at[:, cols], dev(zz=mate), s_w[n])

    def point_rows(zz):
        return pl.ds(pl.multiple_of((x * SIDE + zz) * 16 + 8 * core, 8), 8)

    mgathers = [Gather(mg, n, PIECE) for n in range(PIECES)]
    k_out = [(number(), number()) for _ in range(PIECES)]
    s_out = [(leave(), leave()) for _ in range(PIECES)]
    outs = []

    def rs4(n):
        cols = chunk_cols(n)
        g = mgathers[n]
        ratio = tim[:, cols] / jnp.sum(vr[2, :, :, cols], axis=0)
        keep = 1.0 - tim[:, cols]
        share = rx_sum(n, "z", z, 1)
        mg[point_rows(z), cols] = keep * sg[point_rows(z), cols] + ratio * share
        g.near()
        share = rx_end(n, "o", opp, 0)
        c[n, "last"].wait_recv()
        mg[point_rows(opp), cols] = keep * sg[point_rows(opp), cols] + ratio * (share + qb[:, cols])
        g.far()
        g.far_x()
        here = mv.at[pl.ds(pl.multiple_of(8 * core, 8), 8), cols]
        there = mv.at[pl.ds(pl.multiple_of(8 * other, 8), 8), cols]

        def result(zz, device, k):
            return pltpu.make_async_remote_copy(
                src_ref=slot(mg, 0, zz, core, cols), dst_ref=here, send_sem=send_sem.at[k], recv_sem=recv_sem.at[k_out[n][0] + core],
                device_id=device, device_id_type=MESH,
            )

        far_out = result(opp, dev(zz=opp, cc=block), s_out[n][0])
        near_out = result(z, dev(cc=other), s_out[n][1])
        far_out.start()
        started.append(far_out)

        @pl.when(mine)
        def _():
            here[...] = mg[point_rows(z), cols]

        @pl.when(jnp.logical_not(mine))
        def _():
            near_out.start()

        def result_in(ref, k):
            return pltpu.make_async_remote_copy(
                src_ref=ref, dst_ref=ref, send_sem=send_sem.at[s_out[n][0]], recv_sem=recv_sem.at[k],
                device_id=dev(cc=other), device_id_type=MESH,
            )

        outs.append((near_out, result_in(here, k_out[n][0] + core), result_in(there, k_out[n][0] + other)))

    def gather_on(n):
        mgathers[n].near_on()
        mgathers[n].far_mate()
        mgathers[n].far_on()

    weigh(0)
    weigh(1)
    rs1(0)
    weigh(2)
    rs1(1)
    weigh(3)
    rs2(0)
    rs3(0)
    rs1(2)
    rs2(1)
    rs3(1)
    rs1(3)
    arrived(copies)
    rs4(0)
    rs2(2)
    rs3(2)
    rs4(1)
    gather_on(0)
    rs2(3)
    rs3(3)
    rs4(2)
    gather_on(1)
    rs4(3)
    mgathers[0].last()
    gather_on(2)

    def last_chunk(n):
        def norm(cols, value):
            phi[:, cols] = (f2[:, cols] - value) * SCALE

        split_chunk(mg, n, PIECE, norm)
        cols = slice(n * PIECE, n * PIECE + PIECE)
        scores = jnp.dot(tcat[...], scat[:, cols], preferred_element_type=F32) + phi[:, cols]
        q[:, cols] = scores
        if n == 0:
            nb[...] = lane_top(scores)
        else:
            fresh = jnp.maximum(nb[...], lane_top(scores))
            sb[...] = sb[...] * jnp.exp2(nb[...] - fresh)
            nb[...] = fresh

        def step(r, _):
            rows = pl.ds(pl.multiple_of(r * 8, 8), 8)
            part_sum = tiles(jnp.exp2(q[rows, cols] - wide(nb[rows, :], PIECE // 128)))
            sb[rows, :] = part_sum if n == 0 else sb[rows, :] + part_sum
            return 0

        lax.fori_loop(0, COLS // 8, step, 0, unroll=8)

    def last_lse():
        cb[...] = nb[...]
        join_tops()
        sb[...] = sb[...] * jnp.exp2(cb[...] - nb[...])
        ntop, total = column_lse()
        return ntop + jnp.log(total) * LOG2E

    def results():
        for near_out, half_here, half_there in outs:
            half_there.wait_recv()

            @pl.when(jnp.logical_not(mine))
            def _():
                half_here.wait_recv()
                near_out.wait_send()

        fr[...] = jnp.where(mine, f2[...], ff[...])
        for store in stores[:2]:
            store.start()

    mgathers[0].finish()
    last_chunk(0)
    results()
    mgathers[1].last()
    gather_on(3)
    mgathers[1].finish()
    last_chunk(1)
    mgathers[2].last()
    mgathers[2].finish()
    last_chunk(2)
    mgathers[3].last()
    mgathers[3].finish()
    last_chunk(3)

    home = z + core * (opp - z)
    part[...] = last_lse() - half_t[...] * SCALE

    def to_owner(dy, cc, k, base):
        return pltpu.make_async_remote_copy(
            src_ref=part, dst_ref=vc.at[2, line_slot], send_sem=send_sem.at[k], recv_sem=recv_sem.at[base + core],
            device_id=dev(dy=dy, zz=home, cc=cc), device_id_type=MESH,
        )

    def from_owner(k):
        return copy_to(part, vc.at[2, line_slot], dev(cc=other), k)

    waits = []
    for dy in (2, 1, -1):
        base, more = number(), number()
        for cc in (0, 1):
            copy = to_owner(dy, cc, leave(), base)
            copy.start()
            started.append(copy)
        waits += [from_owner(base), from_owner(more)]
    base, more = number(), number()
    to_one, to_zero = to_owner(0, 1, leave(), base), to_owner(0, 0, leave(), base)
    to_one.start()
    started.append(to_one)

    @pl.when(core == 1)
    def _():
        to_zero.start()
        from_owner(base).wait_recv()

    @pl.when(core == 0)
    def _():
        vc[2, line_slot] = part[...]

    from_owner(more).wait_recv()
    arrived(waits)
    fc[...] = EPSILON * (own[2][:, 0:COLS] - LN2 * lse_over_first(vc[2]))
    stores[2].start()
    for store in stores:
        store.wait()

    @pl.when(core == 1)
    def _():
        to_zero.wait_send()

    for copy in started:
        copy.wait_send()


def per_device(sources, targets, source_logw, target_logw, times):
    anywhere = pl.BlockSpec(memory_space=pl.ANY)
    rowp, moved, colp = pl.pallas_call(
        kernel,
        out_shape=(
            jax.ShapeDtypeStruct((1, ROWS), F32),
            jax.ShapeDtypeStruct((16, ROWS), F32),
            jax.ShapeDtypeStruct((1, COLS), F32),
        ),
        in_specs=[anywhere] * 5,
        out_specs=(anywhere,) * 3,
        scratch_shapes=[
            pltpu.VMEM((16, ROWS), F32),
            pltpu.VMEM((32, COLS), F32),
            pltpu.VMEM((3, 1, ROWS), F32),
            pltpu.VMEM((3, 1, ROWS), F32),
            pltpu.VMEM((1, ROWS), F32),
            pltpu.VMEM((1, COLS), F32),
            pltpu.VMEM((1, ROWS), F32),
            pltpu.VMEM((FEATURES, ROWS), F32),
            pltpu.VMEM((FEATURES, COLS), F32),
            pltpu.VMEM((FEATURES, ROWS), F32),
            pltpu.VMEM((16, ROWS), F32),
            pltpu.VMEM((COLS, 3 * FEATURES), BF16),
            pltpu.VMEM((3 * FEATURES, ROWS), BF16),
            pltpu.VMEM((COLS, ROWS), F32),
            pltpu.VMEM((COLS, ROWS), F32),
            pltpu.VMEM((SIDE, SIDE, 2, 8, ROWS), F32),
            pltpu.VMEM((2 * FEATURES, COLS), BF16),
            pltpu.VMEM((COLS, ROWS), BF16),
            pltpu.VMEM((COLS, ROWS), BF16),
            pltpu.VMEM((SIDE, SIDE, 8, ROWS), F32),
            pltpu.VMEM((SIDE, 8, ROWS), F32),
            pltpu.VMEM((1, 8, ROWS), F32),
            pltpu.VMEM((1, 2, 8, ROWS), F32),
            pltpu.VMEM((2, 3, 8, ROWS), F32),
            pltpu.VMEM((8, ROWS), F32),
            pltpu.VMEM((3, GROUP, 1, ROWS), F32),
            pltpu.VMEM((3, LINE, 1, COLS), F32),
            pltpu.VMEM((COLS, 128), F32),
            pltpu.VMEM((COLS, 128), F32),
            pltpu.VMEM((COLS, 128), F32),
            pltpu.VMEM((1, COLS), F32),
            pltpu.VMEM((1, ROWS), F32),
            pltpu.VMEM((1, ROWS), F32),
            pltpu.VMEM((1, ROWS), F32),
            pltpu.VMEM((1, ROWS), F32),
            pltpu.VMEM((1, ROWS), F32),
            pltpu.VMEM((1, COLS), F32),
            pltpu.VMEM((1, COLS), F32),
            pltpu.SemaphoreType.DMA((DEPARTURES,)),
            pltpu.SemaphoreType.DMA((ARRIVALS,)),
            pltpu.SemaphoreType.DMA((5,)),
        ],
        compiler_params=pltpu.CompilerParams(
            collective_id=0, has_side_effects=True, vmem_limit_bytes=60 * 1024 * 1024
        ),
    )(sources, targets, source_logw[None], target_logw[None], times[None])
    return rowp[0], moved, colp[0]


def solution(mesh):
    return jax.shard_map(
        per_device,
        mesh=mesh,
        in_specs=(P("tgt", "src"), P("src", "tgt"), P("src"), P("tgt"), P("src")),
        out_specs=(P("src"), P("tgt", "src"), P("tgt")),
        check_vma=False,
    )
```

```python
import functools

import jax
import jax.numpy as jnp
from jax import lax
from jax.experimental import pallas as pl
from jax.experimental.pallas import tpu as pltpu
from jax.sharding import PartitionSpec as P

MESH = pl.DeviceIdType.MESH
F32 = jnp.float32
BF16 = jnp.bfloat16
EPSILON = 16.0
LOG2E = 1.4426950408889634
LN2 = 0.6931471805599453
SCALE = LOG2E / EPSILON

FEATURES = 256
ROWS = 2048
COLS = 1024
SIDE = 4
GROUP = 16
LINE = 8
ARRIVALS = 143
DEPARTURES = 44
CHUNKS = 2
CHUNK = ROWS // CHUNKS
PIECES = 4
PIECE = ROWS // PIECES
WIDTH = 256
PARTS = 2
PART = COLS // PARTS
BLOCK = 512


def halves(a):
    high = a.astype(BF16)
    return high, (a - high.astype(F32)).astype(BF16)


def tiles(a):
    return functools.reduce(lambda p, r: p + r, [a[:, 128 * k : 128 * k + 128] for k in range(a.shape[1] // 128)])


def kernel(
    src_h, tgt_h, slw_h, tlw_h, tim_h,
    rowp, moved, colp,
    src, tgt, own, far, slw, tlw, tim, sg, tg, mg, mv, tcat, scat, q, e, w, tw, eh, el,
    r0, rb, rx1, rx2, rd, qb, vr, vc, nb, sb, cb, part, frow, phi, f2, ff, fr, fc, half_t,
    send_sem, recv_sem, in_sem,
):
    me_s, me_t = lax.axis_index("src"), lax.axis_index("tgt")
    x, z = me_t // SIDE, me_t % SIDE
    y, core = me_s // 2, me_s % 2
    block = z // 2
    mate = z + 1 - 2 * (z % 2)
    opp = SIDE - 1 - z
    mates_opp = SIDE - 1 - mate
    other = 1 - core
    mine = core == block
    started = []

    def wrap(value):
        return lax.rem(value + SIDE, SIDE)

    def dev(dx=0, dy=0, zz=z, cc=core):
        return (wrap(y + dy) * 2 + cc, wrap(x + dx) * SIDE + zz)

    def copy_to(source, target, device, k, out=0):
        return pltpu.make_async_remote_copy(
            src_ref=source, dst_ref=target, send_sem=send_sem.at[out], recv_sem=recv_sem.at[k],
            device_id=device, device_id_type=MESH,
        )

    count, leaves = [0], [0]

    def number():
        count[0] += 1
        return count[0] - 1

    def leave():
        leaves[0] += 1
        return leaves[0] - 1

    def send(source, target, device, out=None, k=None):
        copy = copy_to(source, target, device, number() if k is None else k, leave() if out is None else out)
        copy.start()
        if out is None:
            started.append(copy)
        return copy

    def all_left(ref, out):
        started.append(copy_to(ref, ref, dev(cc=other), 0, out))

    loads = [
        pltpu.make_async_copy(a, b, in_sem.at[k])
        for k, (a, b) in enumerate(((src_h, src), (tgt_h, tgt), (slw_h, own.at[0]), (tim_h, own.at[1]), (tlw_h, own.at[2, :, pl.ds(0, COLS)])))
    ]
    for load in loads:
        load.start()
    stores = [pltpu.make_async_copy(a, b, in_sem.at[k]) for k, (a, b) in enumerate(((mv, moved), (fr, rowp), (fc, colp)))]
    barrier = pltpu.get_barrier_semaphore()
    near = [dev(1), dev(-1), dev(2), dev(dy=1), dev(dy=-1), dev(zz=mate), dev(zz=opp), dev(zz=opp, cc=other), dev(cc=other)]
    for device in near:
        pl.semaphore_signal(barrier, inc=1, device_id=device, device_id_type=MESH)
    for load in loads:
        load.wait()
    pl.semaphore_wait(barrier, len(near))

    def slot(buf, dx, zz, cc, cols):
        return buf.at[pl.ds(pl.multiple_of((wrap(x + dx) * SIDE + zz) * 16 + 8 * cc, 8), 8), cols]

    def chunk_cols(n, size=PIECE):
        return pl.ds(n * size, size)

    def chunk_half(n, d, size=PIECE):
        return pl.ds(n * size + (0 if d == 1 else size // 2), size // 2)

    class Gather:
        def __init__(self, buf, n, size):
            self.buf, self.n, self.size = buf, n, size
            self.cols = chunk_cols(n, size)
            self.c = {}
            self.out, self.shared = leave(), number()
            self.from_mate, self.second, self.third = number(), number(), number()
            all_left(buf.at[0:240, self.cols], self.out)

        def share(self, dx, zz):
            ref = slot(self.buf, dx, zz, core, self.cols)
            send(ref, ref, dev(cc=other), self.out, self.shared)

        def to_mate(self, key, dx, zz, k=None):
            ref = slot(self.buf, dx, zz, core, self.cols)
            self.c[key] = send(ref, ref, dev(zz=mate), self.out, k)

        def round_x(self, key, zz, shifts, k=None):
            ref = slot(self.buf, 0, zz, core, self.cols)
            for d in shifts:
                self.c[key, d] = send(ref, ref, dev(d), self.out, k)

        def near(self):
            self.round_x("n", z, (2, 1, -1))
            self.to_mate(("m", 0), 0, z)
            self.share(0, z)

        def far(self, pass_on=True):
            if pass_on:
                self.to_mate("fm", 0, opp)
            self.share(0, opp)

        def far_x(self):
            self.round_x("f", opp, (1, -1))

        def near_on(self):
            for d in (1, -1, 2):
                self.c["n", d].wait_recv()
                self.to_mate(("m", -d), -d, z, self.from_mate)
                self.share(-d, z)

        def far_mate(self):
            if "fm" in self.c:
                self.c["fm"].wait_recv()
            self.round_x("g", mates_opp, (2, 1, -1), self.third)
            self.share(0, mates_opp)

        def far_on(self):
            for d in (1, -1):
                self.c["f", d].wait_recv()
                ref = slot(self.buf, -d, opp, core, chunk_half(self.n, d, self.size))
                send(ref, ref, dev(d), self.out, self.second)
                self.share(-d, opp)

        def last(self):
            self.c["m", 0].wait_recv()
            self.share(0, mate)
            self.rows_in(8, self.second)
            self.share(2, opp)
            self.rows_in(24, self.from_mate)
            for dx in (1, -1, 2):
                self.share(dx, mate)
            self.rows_in(24, self.third)
            for dx in (1, -1, 2):
                self.share(dx, mates_opp)

        def rows_in(self, rows, k):
            ref = self.buf.at[0:rows, self.cols]
            copy_to(ref, ref, dev(cc=other), k).wait_recv()

        def finish(self):
            self.rows_in(128, self.shared)

    def group_devices():
        return [
            dev(dx, zz=zz, cc=cc)
            for dx in (2, 1, -1, 0)
            for zz in (mate, z)
            for cc in (other, core)
            if not (dx == 0 and zz is z and cc is core)
        ]

    group_slot = x * 4 + (z % 2) * 2 + core
    line_slot = y * 2 + block

    def to_all(buf, k, row, devices):
        buf[k] = row
        out, arrival = leave(), number()
        for device in devices:
            send(buf.at[k], buf.at[k], device, out, arrival)
        whole = buf.at[0 : len(devices)]
        all_left(whole, out)
        return [copy_to(whole, whole, dev(cc=other), arrival)]

    def to_group(buf, row):
        return to_all(buf, group_slot, row, group_devices())

    line = [(dy, zz, cc) for dy in (2, 1, -1, 0) for zz, cc in ((opp, other), (z, core)) if not (dy == 0 and zz is z)]

    def to_line(buf, row):
        return to_all(buf, line_slot, row, [dev(dy=dy, zz=zz, cc=cc) for dy, zz, cc in line])

    def arrived(copies):
        for copy in copies:
            copy.wait_recv()

    def lse_over_first(a):
        top = jnp.max(a, axis=0)
        return top + jnp.log(jnp.sum(jnp.exp2(a - top[None]), axis=0)) * LOG2E

    def as_column(row, ref):
        for b in range(COLS // 128):
            piece = row[:, 128 * b : 128 * b + 128]
            ref[128 * b : 128 * b + 128, :] = jnp.broadcast_to(piece, (128, 128)).T

    def column_top(ref):
        return jnp.concatenate([ref[128 * b : 128 * b + 128, :].T[0:1, :] for b in range(COLS // 128)], axis=1)

    def column_sum(ref):
        return jnp.concatenate(
            [jnp.sum(ref[128 * b : 128 * b + 128, :].T, axis=0, keepdims=True) for b in range(COLS // 128)], axis=1
        )

    both = pl.ds(0, ROWS)
    k_near, s_near = number(), leave()
    k_far, s_far = number(), (leave(), leave())

    def out_half(cc):
        return src.at[pl.ds(pl.multiple_of(8 * cc, 8), 8), :]

    give_near = copy_to(out_half(other), slot(sg, 0, z, other, both), dev(cc=other), k_near, s_near)
    give_far = [copy_to(out_half(cc), slot(sg, 0, z, cc, both), dev(zz=opp, cc=cc), k_far, s_far[cc]) for cc in (0, 1)]
    take_near = copy_to(out_half(0), slot(sg, 0, z, core, both), dev(cc=other), k_near)
    take_far = copy_to(out_half(0), slot(sg, 0, opp, core, both), dev(zz=opp), k_far)

    k_t = [(number(), number()) for _ in range(PARTS)]
    s_t = [(leave(), leave()) for _ in range(PARTS)]
    parts = [pl.ds(k * PART, PART) for k in range(PARTS)]

    def tslot(dy, cc, rows=None, cols=slice(None)):
        start, size = (0, 32) if rows is None else rows
        return tg.at[pl.ds(pl.multiple_of(64 * wrap(y + dy) + 32 * cc + start, 16), size), cols]

    def tcopy(device, k, which):
        return pltpu.make_async_remote_copy(
            src_ref=tgt.at[:, parts[k]], dst_ref=tslot(0, core, cols=parts[k]),
            send_sem=send_sem.at[s_t[k][which]], recv_sem=recv_sem.at[k_t[k][0] + core],
            device_id=device, device_id_type=MESH,
        )

    give_t = [tcopy(dev(zz=opp, cc=1), k, 0) for k in range(PARTS)]
    give_t_here = [tcopy(dev(cc=0), k, 1) for k in range(PARTS)]
    take_t = [
        [copy_to(tgt.at[:, parts[k]], tslot(0, cc, cols=parts[k]), dev(zz=opp, cc=1), k_t[k][cc]) for cc in (0, 1)]
        for k in range(PARTS)
    ]

    def targets_out(k):
        give_t[k].start()

        @pl.when(core == 1)
        def _():
            give_t_here[k].start()

    targets_out(0)

    @pl.when(mine)
    def _():
        give_near.start()

    @pl.when(jnp.logical_not(mine))
    def _():
        give_far[0].start()
        give_far[1].start()

    for k in range(1, PARTS):
        targets_out(k)
    small = [
        send(own.at[0], far.at[0], dev(cc=other)),
        send(own.at[1], far.at[1], dev(cc=other)),
        send(own.at[2, :, pl.ds(0, COLS)], far.at[2, :, pl.ds(0, COLS)], dev(zz=opp)),
    ]

    @pl.when(mine)
    def _():
        slot(sg, 0, z, core, both)[...] = out_half(core)[...]

    @pl.when(core == 0)
    def _():
        tslot(0, 0)[...] = tgt[...]

    @pl.when(jnp.logical_not(mine))
    def _():
        take_near.wait_recv()

    gathers = [Gather(sg, n, CHUNK) for n in range(CHUNKS)]
    for g in gathers:
        g.near()

    yc = {}
    s_y = [leave() for _ in range(PARTS)]
    for k in range(PARTS):
        all_left(tg.at[0:192, parts[k]], s_y[k])

    k_f = [number() for _ in range(PARTS)]

    def targets_start(k):
        for cc in (0, 1):
            if cc == 0:

                @pl.when(core == 1)
                def _():
                    take_t[k][0].wait_recv()
            else:
                take_t[k][1].wait_recv()
            ref = tslot(0, cc, cols=parts[k])
            for d in (1, -1):
                yc[k, cc, d] = send(ref, ref, dev(dy=d), s_y[k])

    targets_start(0)
    take_far.wait_recv()
    for g in gathers:
        g.far()
    for g in gathers:
        g.far_x()

    def targets_on(k):
        for cc in (0, 1):
            for d in (1, -1):
                yc[k, cc, d].wait_recv()
                ref = tslot(-d, cc, (0 if d == 1 else 16, 16), parts[k])
                send(ref, ref, dev(dy=d), s_y[k], k_f[k])

    def targets_in(k):
        ref = tg.at[0:64, parts[k]]
        copy_to(ref, ref, dev(dy=1), k_f[k]).wait_recv()
        cols = slice(k * PART, k * PART + PART)
        half_t[:, cols] = 0.5 * jnp.sum(tg[:, cols] * tg[:, cols], axis=0, keepdims=True)
        for b in range(k * PART // 128, (k + 1) * PART // 128):
            here = slice(128 * b, 128 * b + 128)
            high, low = halves(tg[:, here].T * SCALE)
            tcat[here, 0:256] = high
            tcat[here, 256:512] = high
            tcat[here, 512:768] = low
            cb[here, :] = jnp.broadcast_to(half_t[:, here] * SCALE, (128, 128)).T

    gathers[0].near_on()
    for k in range(1, PARTS):
        targets_start(k)
    for g in gathers[1:]:
        g.near_on()
    targets_on(0)
    for g in gathers:
        g.far_mate()
        g.far_on()
    for k in range(1, PARTS):
        targets_on(k)
    gathers[0].last()
    targets_in(0)

    def split_points(buf, n):
        cols = pl.ds(pl.multiple_of(n * WIDTH, WIDTH), WIDTH)
        a = buf[:, cols]
        high, low = halves(a)
        scat[0:256, cols] = high
        scat[256:512, cols] = low
        scat[512:768, cols] = high
        return 0.5 * jnp.sum(a * a, axis=0, keepdims=True)

    def split_chunk(buf, n, size, norm):
        def step(m, _):
            cols = pl.ds(pl.multiple_of(m * WIDTH, WIDTH), WIDTH)
            norm(cols, split_points(buf, m))
            return 0

        lax.fori_loop(n * size // WIDTH, (n + 1) * size // WIDTH, step, 0)

    def blocks(n, size):
        return [slice(k, k + BLOCK) for k in range(n * size, (n + 1) * size, BLOCK)]

    def wide(a, pieces):
        return jnp.concatenate([a] * pieces, axis=1)

    def lane_top(a):
        return functools.reduce(jnp.maximum, [a[:, k : k + 128] for k in range(0, a.shape[1], 128)])

    def row_pass(body, first=0, size=COLS):
        def step(r, acc):
            return acc + body(pl.ds(pl.multiple_of(r * 8, 8), 8))

        acc = lax.fori_loop(first // 8, (first + size) // 8, step, jnp.zeros((8, ROWS), F32), unroll=4)
        return jnp.sum(acc, axis=0, keepdims=True)

    row_lse = []
    for k in range(PARTS):
        here = slice(k * PART, k * PART + PART)
        if k > 0:
            targets_in(k)

        for n, g in enumerate(gathers):
            if k == 0:
                if n > 0:
                    g.last()
                g.finish()

                def norm(cols, value):
                    frow[:, cols] = value

                split_chunk(sg, n, CHUNK, norm)
            for cols in blocks(n, CHUNK):
                cross = jnp.dot(tcat[here, :], scat[:, cols], preferred_element_type=F32)
                q[here, cols] = cross
                phi[:, cols] = jnp.max(cross - wide(cb[here, :], BLOCK // 128), axis=0, keepdims=True)
        top = phi[...]
        row_lse.append(top + jnp.log(row_pass(lambda rows: jnp.exp2(q[rows, :] - wide(cb[rows, :], ROWS // 128) - top), k * PART, PART)) * LOG2E)

    arrived(small)
    slw[...] = jnp.where(mine, own[0], far[0])
    tim[...] = jnp.where(mine, own[1], far[1])
    tlw[...] = jnp.where(core == 0, own[2], far[2])[:, 0:COLS]

    for k in range(PARTS):
        give_t[k].wait_send()

    @pl.when(core == 1)
    def _():
        for k in range(PARTS):
            give_t_here[k].wait_send()

    @pl.when(mine)
    def _():
        give_near.wait_send()

    @pl.when(jnp.logical_not(mine))
    def _():
        give_far[0].wait_send()
        give_far[1].wait_send()

    copies = to_group(vr.at[0], lse_over_first(jnp.stack(row_lse)))
    arrived(copies)
    lse = lse_over_first(vr[0])
    phi[...] = slw[...] * LOG2E - lse
    frow[...] = frow[...] + EPSILON * (slw[...] - LN2 * lse)

    def join_tops():
        for b in range(0, COLS, 128):
            nb[b : b + 128, :] = jnp.broadcast_to(jnp.max(nb[b : b + 128, :], axis=1, keepdims=True), (128, 128))

    def top_step(r, _):
        rows = pl.ds(pl.multiple_of(r * 8, 8), 8)
        nb[rows, :] = lane_top(q[rows, :] + phi[...])
        return 0

    def exp_step(r, _):
        rows = pl.ds(pl.multiple_of(r * 8, 8), 8)
        p = jnp.exp2(q[rows, :] + phi[...] - wide(nb[rows, :], ROWS // 128))
        e[rows, :] = p
        sb[rows, :] = tiles(p)
        return 0

    def column_lse():
        return column_top(nb), column_sum(sb)

    lax.fori_loop(0, COLS // 8, top_step, 0, unroll=4)
    join_tops()
    lax.fori_loop(0, COLS // 8, exp_step, 0, unroll=4)
    ntop, total = column_lse()
    copies = to_line(vc.at[0], ntop + jnp.log(total) * LOG2E)

    def split_step(r, _):
        rows = pl.ds(pl.multiple_of(r * 16, 16), 16)
        high, low = halves(e[rows, :])
        eh[rows, :] = high
        el[rows, :] = low
        return 0

    lax.fori_loop(0, COLS // 16, split_step, 0, unroll=2)
    arrived(copies)
    factor = jnp.exp2(ntop + (tlw[...] * LOG2E - lse_over_first(vc[0])))
    as_column(factor, cb)

    def against_column(rows):
        return e[rows, :] * wide(cb[rows, :], ROWS // 128)

    copies = to_group(vr.at[1], row_pass(against_column))
    arrived(copies)
    total = jnp.sum(vr[1], axis=0)
    f2[...] = frow[...] + EPSILON * (slw[...] - jnp.log(total))
    phi[...] = jnp.exp(slw[...]) / total
    potential = send(f2, ff, dev(zz=opp))

    def weigh_step(r, _):
        rows = pl.ds(pl.multiple_of(r * 8, 8), 8)
        sb[rows, :] = tiles(e[rows, :] * phi[...])
        return 0

    lax.fori_loop(0, COLS // 8, weigh_step, 0, unroll=4)
    copies = to_line(vc.at[1], factor * column_sum(sb))
    arrived(copies)
    dual = factor * (jnp.exp(tlw[...]) / jnp.sum(vc[1], axis=0))

    potential.wait_recv()

    high, low = halves(tg[...] * dual)
    tw[0:256, :] = high
    tw[256:512, :] = low
    def wz(zz, cols, dx=None):
        return w.at[slice(None) if dx is None else wrap(x + dx), zz, core, :, cols]

    c = {}

    s_w = [leave() for _ in range(PIECES)]
    for n in range(PIECES):
        all_left(mg.at[0:240, chunk_cols(n)], s_w[n])

    def weigh(m):
        cols = slice(m * PIECE, m * PIECE + PIECE)
        acc = jnp.dot(tw[0:256, :], eh[:, cols], preferred_element_type=F32)
        acc = acc + jnp.dot(tw[0:256, :], el[:, cols], preferred_element_type=F32)
        acc = acc + jnp.dot(tw[256:512, :], eh[:, cols], preferred_element_type=F32)
        w[:, :, :, :, cols] = acc.reshape(SIDE, SIDE, 2, 8, PIECE)
        c[m, "core"] = send(w.at[:, :, other, :, cols], r0.at[:, :, :, cols], dev(cc=other), s_w[m])

    def rx_start(n, key, zz, k):
        for d in (1, -1):
            cut = chunk_half(n, d)
            c[n, key, d] = send(wz(zz, cut, 2), rx1.at[k, :, cut], dev(d), s_w[n])

    def rx_middle(n, key, zz, k):
        for d in (1, -1):
            cut = chunk_half(n, d)
            c[n, key, d].wait_recv()
            ref = wz(zz, cut, d)
            ref[...] = ref[...] + rx1[k, :, cut]
            c[n, key, "s", d] = send(wz(zz, chunk_cols(n), d), rx2.at[k, 0 if d == 1 else 1, :, chunk_cols(n)], dev(d), s_w[n])

    def rx_end(n, key, zz, k):
        for d in (1, -1):
            c[n, key, "s", d].wait_recv()
        cols = chunk_cols(n)
        return wz(zz, cols, 0)[...] + rx2[k, 0, :, cols] + rx2[k, 1, :, cols]

    def rx_direct(n, key, zz, k):
        c[n, key] = number()
        for i, d in enumerate((2, 1, -1)):
            send(wz(zz, chunk_cols(n), d), rd.at[k, i, :, chunk_cols(n)], dev(d), s_w[n], c[n, key])

    def rx_sum(n, key, zz, k):
        cols = chunk_cols(n)
        ref = rd.at[k, :, :, cols]
        copy_to(ref, ref, dev(1), c[n, key]).wait_recv()
        return wz(zz, cols, 0)[...] + rd[k, 0, :, cols] + rd[k, 1, :, cols] + rd[k, 2, :, cols]

    def rs1(n):
        cols = chunk_cols(n)
        c[n, "core"].wait_recv()
        ref = w.at[:, :, core, :, cols]
        ref[...] = ref[...] + r0[:, :, :, cols]
        c[n, "mate"] = send(wz(mate, cols), rb.at[:, :, cols], dev(zz=mate), s_w[n])
        rx_direct(n, "m", mates_opp, 0)
        rx_start(n, "o", opp, 0)

    def rs2(n):
        cols = chunk_cols(n)
        c[n, "mate"].wait_recv()
        ref = wz(z, cols)
        ref[...] = ref[...] + rb[:, :, cols]
        rx_direct(n, "z", z, 1)
        rx_middle(n, "o", opp, 0)

    def rs3(n):
        cols = chunk_cols(n)
        qs = wz(mates_opp, cols, 0)
        qs[...] = rx_sum(n, "m", mates_opp, 0)
        c[n, "last"] = send(qs, qb.at[:, cols], dev(zz=mate), s_w[n])

    def point_rows(zz):
        return pl.ds(pl.multiple_of((x * SIDE + zz) * 16 + 8 * core, 8), 8)

    mgathers = [Gather(mg, n, PIECE) for n in range(PIECES)]
    k_out = [(number(), number()) for _ in range(PIECES)]
    s_out = [(leave(), leave()) for _ in range(PIECES)]
    outs = []

    def rs4(n):
        cols = chunk_cols(n)
        g = mgathers[n]
        ratio = tim[:, cols] / jnp.sum(vr[2, :, :, cols], axis=0)
        keep = 1.0 - tim[:, cols]
        share = rx_sum(n, "z", z, 1)
        mg[point_rows(z), cols] = keep * sg[point_rows(z), cols] + ratio * share
        g.near()
        share = rx_end(n, "o", opp, 0)
        c[n, "last"].wait_recv()
        mg[point_rows(opp), cols] = keep * sg[point_rows(opp), cols] + ratio * (share + qb[:, cols])
        g.far()
        g.far_x()
        here = mv.at[pl.ds(pl.multiple_of(8 * core, 8), 8), cols]
        there = mv.at[pl.ds(pl.multiple_of(8 * other, 8), 8), cols]

        def result(zz, device, k):
            return pltpu.make_async_remote_copy(
                src_ref=slot(mg, 0, zz, core, cols), dst_ref=here, send_sem=send_sem.at[k], recv_sem=recv_sem.at[k_out[n][0] + core],
                device_id=device, device_id_type=MESH,
            )

        far_out = result(opp, dev(zz=opp, cc=block), s_out[n][0])
        near_out = result(z, dev(cc=other), s_out[n][1])
        far_out.start()
        started.append(far_out)

        @pl.when(mine)
        def _():
            here[...] = mg[point_rows(z), cols]

        @pl.when(jnp.logical_not(mine))
        def _():
            near_out.start()

        def result_in(ref, k):
            return pltpu.make_async_remote_copy(
                src_ref=ref, dst_ref=ref, send_sem=send_sem.at[s_out[n][0]], recv_sem=recv_sem.at[k],
                device_id=dev(cc=other), device_id_type=MESH,
            )

        outs.append((near_out, result_in(here, k_out[n][0] + core), result_in(there, k_out[n][0] + other)))

    def gather_on(n):
        mgathers[n].near_on()
        mgathers[n].far_mate()
        mgathers[n].far_on()

    weigh(0)
    weigh(1)
    rs1(0)
    as_column(dual, cb)
    copies = to_group(vr.at[2], row_pass(against_column))
    weigh(2)
    rs1(1)
    weigh(3)
    rs2(0)
    rs3(0)
    rs1(2)
    rs2(1)
    rs3(1)
    rs1(3)
    arrived(copies)
    rs4(0)
    rs2(2)
    rs3(2)
    rs4(1)
    gather_on(0)
    rs2(3)
    rs3(3)
    rs4(2)
    gather_on(1)
    rs4(3)
    mgathers[0].last()
    gather_on(2)

    def last_chunk(n):
        def norm(cols, value):
            phi[:, cols] = (f2[:, cols] - value) * SCALE

        split_chunk(mg, n, PIECE, norm)
        cols = slice(n * PIECE, n * PIECE + PIECE)
        scores = jnp.dot(tcat[...], scat[:, cols], preferred_element_type=F32) + phi[:, cols]
        q[:, cols] = scores
        if n == 0:
            nb[...] = lane_top(scores)
        else:
            fresh = jnp.maximum(nb[...], lane_top(scores))
            sb[...] = sb[...] * jnp.exp2(nb[...] - fresh)
            nb[...] = fresh

        def step(r, _):
            rows = pl.ds(pl.multiple_of(r * 8, 8), 8)
            part_sum = tiles(jnp.exp2(q[rows, cols] - wide(nb[rows, :], PIECE // 128)))
            sb[rows, :] = part_sum if n == 0 else sb[rows, :] + part_sum
            return 0

        lax.fori_loop(0, COLS // 8, step, 0, unroll=8)

    def last_lse():
        cb[...] = nb[...]
        join_tops()
        sb[...] = sb[...] * jnp.exp2(cb[...] - nb[...])
        ntop, total = column_lse()
        return ntop + jnp.log(total) * LOG2E

    def results():
        for near_out, half_here, half_there in outs:
            half_there.wait_recv()

            @pl.when(jnp.logical_not(mine))
            def _():
                half_here.wait_recv()
                near_out.wait_send()

        fr[...] = jnp.where(mine, f2[...], ff[...])
        for store in stores[:2]:
            store.start()

    mgathers[0].finish()
    last_chunk(0)
    results()
    mgathers[1].last()
    gather_on(3)
    mgathers[1].finish()
    last_chunk(1)
    mgathers[2].last()
    mgathers[2].finish()
    last_chunk(2)
    mgathers[3].last()
    mgathers[3].finish()
    last_chunk(3)

    home = z + core * (opp - z)
    part[...] = last_lse() - half_t[...] * SCALE

    def to_owner(dy, cc, k, base):
        return pltpu.make_async_remote_copy(
            src_ref=part, dst_ref=vc.at[2, line_slot], send_sem=send_sem.at[k], recv_sem=recv_sem.at[base + core],
            device_id=dev(dy=dy, zz=home, cc=cc), device_id_type=MESH,
        )

    def from_owner(k):
        return copy_to(part, vc.at[2, line_slot], dev(cc=other), k)

    waits = []
    for dy in (2, 1, -1):
        base, more = number(), number()
        for cc in (0, 1):
            copy = to_owner(dy, cc, leave(), base)
            copy.start()
            started.append(copy)
        waits += [from_owner(base), from_owner(more)]
    base, more = number(), number()
    to_one, to_zero = to_owner(0, 1, leave(), base), to_owner(0, 0, leave(), base)
    to_one.start()
    started.append(to_one)

    @pl.when(core == 1)
    def _():
        to_zero.start()
        from_owner(base).wait_recv()

    @pl.when(core == 0)
    def _():
        vc[2, line_slot] = part[...]

    from_owner(more).wait_recv()
    arrived(waits)
    fc[...] = EPSILON * (own[2][:, 0:COLS] - LN2 * lse_over_first(vc[2]))
    stores[2].start()
    for store in stores:
        store.wait()

    @pl.when(core == 1)
    def _():
        to_zero.wait_send()

    for copy in started:
        copy.wait_send()


def per_device(sources, targets, source_logw, target_logw, times):
    anywhere = pl.BlockSpec(memory_space=pl.ANY)
    rowp, moved, colp = pl.pallas_call(
        kernel,
        out_shape=(
            jax.ShapeDtypeStruct((1, ROWS), F32),
            jax.ShapeDtypeStruct((16, ROWS), F32),
            jax.ShapeDtypeStruct((1, COLS), F32),
        ),
        in_specs=[anywhere] * 5,
        out_specs=(anywhere,) * 3,
        scratch_shapes=[
            pltpu.VMEM((16, ROWS), F32),
            pltpu.VMEM((32, COLS), F32),
            pltpu.VMEM((3, 1, ROWS), F32),
            pltpu.VMEM((3, 1, ROWS), F32),
            pltpu.VMEM((1, ROWS), F32),
            pltpu.VMEM((1, COLS), F32),
            pltpu.VMEM((1, ROWS), F32),
            pltpu.VMEM((FEATURES, ROWS), F32),
            pltpu.VMEM((FEATURES, COLS), F32),
            pltpu.VMEM((FEATURES, ROWS), F32),
            pltpu.VMEM((16, ROWS), F32),
            pltpu.VMEM((COLS, 3 * FEATURES), BF16),
            pltpu.VMEM((3 * FEATURES, ROWS), BF16),
            pltpu.VMEM((COLS, ROWS), F32),
            pltpu.VMEM((COLS, ROWS), F32),
            pltpu.VMEM((SIDE, SIDE, 2, 8, ROWS), F32),
            pltpu.VMEM((2 * FEATURES, COLS), BF16),
            pltpu.VMEM((COLS, ROWS), BF16),
            pltpu.VMEM((COLS, ROWS), BF16),
            pltpu.VMEM((SIDE, SIDE, 8, ROWS), F32),
            pltpu.VMEM((SIDE, 8, ROWS), F32),
            pltpu.VMEM((1, 8, ROWS), F32),
            pltpu.VMEM((1, 2, 8, ROWS), F32),
            pltpu.VMEM((2, 3, 8, ROWS), F32),
            pltpu.VMEM((8, ROWS), F32),
            pltpu.VMEM((3, GROUP, 1, ROWS), F32),
            pltpu.VMEM((3, LINE, 1, COLS), F32),
            pltpu.VMEM((COLS, 128), F32),
            pltpu.VMEM((COLS, 128), F32),
            pltpu.VMEM((COLS, 128), F32),
            pltpu.VMEM((1, COLS), F32),
            pltpu.VMEM((1, ROWS), F32),
            pltpu.VMEM((1, ROWS), F32),
            pltpu.VMEM((1, ROWS), F32),
            pltpu.VMEM((1, ROWS), F32),
            pltpu.VMEM((1, ROWS), F32),
            pltpu.VMEM((1, COLS), F32),
            pltpu.VMEM((1, COLS), F32),
            pltpu.SemaphoreType.DMA((DEPARTURES,)),
            pltpu.SemaphoreType.DMA((ARRIVALS,)),
            pltpu.SemaphoreType.DMA((5,)),
        ],
        compiler_params=pltpu.CompilerParams(
            collective_id=0, has_side_effects=True, vmem_limit_bytes=60 * 1024 * 1024
        ),
    )(sources, targets, source_logw[None], target_logw[None], times[None])
    return rowp[0], moved, colp[0]


def solution(mesh):
    return jax.shard_map(
        per_device,
        mesh=mesh,
        in_specs=(P("tgt", "src"), P("src", "tgt"), P("src"), P("tgt"), P("src")),
        out_specs=(P("src"), P("tgt", "src"), P("tgt")),
        check_vma=False,
    )
```

```python
import functools

import jax
import jax.numpy as jnp
from jax import lax
from jax.experimental import pallas as pl
from jax.experimental.pallas import tpu as pltpu
from jax.sharding import PartitionSpec as P

MESH = pl.DeviceIdType.MESH
F32 = jnp.float32
BF16 = jnp.bfloat16
EPSILON = 16.0
LOG2E = 1.4426950408889634
LN2 = 0.6931471805599453
SCALE = LOG2E / EPSILON

FEATURES = 256
ROWS = 2048
COLS = 1024
SIDE = 4
GROUP = 16
LINE = 8
ARRIVALS = 143
DEPARTURES = 44
CHUNKS = 2
CHUNK = ROWS // CHUNKS
PIECES = 4
PIECE = ROWS // PIECES
WIDTH = 256
PARTS = 2
PART = COLS // PARTS
BLOCK = 512


def halves(a):
    high = a.astype(BF16)
    return high, (a - high.astype(F32)).astype(BF16)


def tiles(a):
    return functools.reduce(lambda p, r: p + r, [a[:, 128 * k : 128 * k + 128] for k in range(a.shape[1] // 128)])


def kernel(
    src_h, tgt_h, slw_h, tlw_h, tim_h,
    rowp, moved, colp,
    src, tgt, own, far, slw, tlw, tim, sg, tg, mg, mv, tcat, scat, q, e, w, tw, eh, el,
    r0, rb, rx1, rx2, rd, qb, vr, vc, nb, sb, cb, part, frow, phi, f2, ff, fr, fc, half_t,
    send_sem, recv_sem, in_sem,
):
    me_s, me_t = lax.axis_index("src"), lax.axis_index("tgt")
    x, z = me_t // SIDE, me_t % SIDE
    y, core = me_s // 2, me_s % 2
    block = z // 2
    mate = z + 1 - 2 * (z % 2)
    opp = SIDE - 1 - z
    mates_opp = SIDE - 1 - mate
    other = 1 - core
    mine = core == block
    started = []

    def wrap(value):
        return lax.rem(value + SIDE, SIDE)

    def dev(dx=0, dy=0, zz=z, cc=core):
        return (wrap(y + dy) * 2 + cc, wrap(x + dx) * SIDE + zz)

    def copy_to(source, target, device, k, out=0):
        return pltpu.make_async_remote_copy(
            src_ref=source, dst_ref=target, send_sem=send_sem.at[out], recv_sem=recv_sem.at[k],
            device_id=device, device_id_type=MESH,
        )

    count, leaves = [0], [0]

    def number():
        count[0] += 1
        return count[0] - 1

    def leave():
        leaves[0] += 1
        return leaves[0] - 1

    def send(source, target, device, out=None, k=None):
        copy = copy_to(source, target, device, number() if k is None else k, leave() if out is None else out)
        copy.start()
        if out is None:
            started.append(copy)
        return copy

    def all_left(ref, out):
        started.append(copy_to(ref, ref, dev(cc=other), 0, out))

    loads = [
        pltpu.make_async_copy(a, b, in_sem.at[k])
        for k, (a, b) in enumerate(((src_h, src), (tgt_h, tgt), (slw_h, own.at[0]), (tim_h, own.at[1]), (tlw_h, own.at[2, :, pl.ds(0, COLS)])))
    ]
    for load in loads:
        load.start()
    stores = [pltpu.make_async_copy(a, b, in_sem.at[k]) for k, (a, b) in enumerate(((mv, moved), (fr, rowp), (fc, colp)))]
    barrier = pltpu.get_barrier_semaphore()
    near = [dev(1), dev(-1), dev(2), dev(dy=1), dev(dy=-1), dev(zz=mate), dev(zz=opp), dev(zz=opp, cc=other), dev(cc=other)]
    for device in near:
        pl.semaphore_signal(barrier, inc=1, device_id=device, device_id_type=MESH)
    for load in loads:
        load.wait()
    pl.semaphore_wait(barrier, len(near))

    def slot(buf, dx, zz, cc, cols):
        return buf.at[pl.ds(pl.multiple_of((wrap(x + dx) * SIDE + zz) * 16 + 8 * cc, 8), 8), cols]

    def chunk_cols(n, size=PIECE):
        return pl.ds(n * size, size)

    def chunk_half(n, d, size=PIECE):
        return pl.ds(n * size + (0 if d == 1 else size // 2), size // 2)

    class Gather:
        def __init__(self, buf, n, size):
            self.buf, self.n, self.size = buf, n, size
            self.cols = chunk_cols(n, size)
            self.c = {}
            self.out, self.shared = leave(), number()
            self.from_mate, self.second, self.third = number(), number(), number()
            all_left(buf.at[0:240, self.cols], self.out)

        def share(self, dx, zz):
            ref = slot(self.buf, dx, zz, core, self.cols)
            send(ref, ref, dev(cc=other), self.out, self.shared)

        def to_mate(self, key, dx, zz, k=None):
            ref = slot(self.buf, dx, zz, core, self.cols)
            self.c[key] = send(ref, ref, dev(zz=mate), self.out, k)

        def round_x(self, key, zz, shifts, k=None):
            ref = slot(self.buf, 0, zz, core, self.cols)
            for d in shifts:
                self.c[key, d] = send(ref, ref, dev(d), self.out, k)

        def near(self):
            self.round_x("n", z, (2, 1, -1))
            self.to_mate(("m", 0), 0, z)
            self.share(0, z)

        def far(self, pass_on=True):
            if pass_on:
                self.to_mate("fm", 0, opp)
            self.share(0, opp)

        def far_x(self):
            self.round_x("f", opp, (1, -1))

        def near_on(self):
            for d in (1, -1, 2):
                self.c["n", d].wait_recv()
                self.to_mate(("m", -d), -d, z, self.from_mate)
                self.share(-d, z)

        def far_mate(self):
            if "fm" in self.c:
                self.c["fm"].wait_recv()
            self.round_x("g", mates_opp, (2, 1, -1), self.third)
            self.share(0, mates_opp)

        def far_on(self):
            for d in (1, -1):
                self.c["f", d].wait_recv()
                ref = slot(self.buf, -d, opp, core, chunk_half(self.n, d, self.size))
                send(ref, ref, dev(d), self.out, self.second)
                self.share(-d, opp)

        def last(self):
            self.c["m", 0].wait_recv()
            self.share(0, mate)
            self.rows_in(8, self.second)
            self.share(2, opp)
            self.rows_in(24, self.from_mate)
            for dx in (1, -1, 2):
                self.share(dx, mate)
            self.rows_in(24, self.third)
            for dx in (1, -1, 2):
                self.share(dx, mates_opp)

        def rows_in(self, rows, k):
            ref = self.buf.at[0:rows, self.cols]
            copy_to(ref, ref, dev(cc=other), k).wait_recv()

        def finish(self):
            self.rows_in(128, self.shared)

    def group_devices():
        return [
            dev(dx, zz=zz, cc=cc)
            for dx in (2, 1, -1, 0)
            for zz in (mate, z)
            for cc in (other, core)
            if not (dx == 0 and zz is z and cc is core)
        ]

    group_slot = x * 4 + (z % 2) * 2 + core
    line_slot = y * 2 + block

    def to_all(buf, k, row, devices):
        buf[k] = row
        out, arrival = leave(), number()
        for device in devices:
            send(buf.at[k], buf.at[k], device, out, arrival)
        whole = buf.at[0 : len(devices)]
        all_left(whole, out)
        return [copy_to(whole, whole, dev(cc=other), arrival)]

    def to_group(buf, row):
        return to_all(buf, group_slot, row, group_devices())

    line = [(dy, zz, cc) for dy in (2, 1, -1, 0) for zz, cc in ((opp, other), (z, core)) if not (dy == 0 and zz is z)]

    def to_line(buf, row):
        return to_all(buf, line_slot, row, [dev(dy=dy, zz=zz, cc=cc) for dy, zz, cc in line])

    def arrived(copies):
        for copy in copies:
            copy.wait_recv()

    def lse_over_first(a):
        top = jnp.max(a, axis=0)
        return top + jnp.log(jnp.sum(jnp.exp2(a - top[None]), axis=0)) * LOG2E

    def as_column(row, ref):
        for b in range(COLS // 128):
            piece = row[:, 128 * b : 128 * b + 128]
            ref[128 * b : 128 * b + 128, :] = jnp.broadcast_to(piece, (128, 128)).T

    def column_top(ref):
        return jnp.concatenate([ref[128 * b : 128 * b + 128, :].T[0:1, :] for b in range(COLS // 128)], axis=1)

    def column_sum(ref):
        return jnp.concatenate(
            [jnp.sum(ref[128 * b : 128 * b + 128, :].T, axis=0, keepdims=True) for b in range(COLS // 128)], axis=1
        )

    both = pl.ds(0, ROWS)
    k_near, s_near = number(), leave()
    k_far, s_far = number(), (leave(), leave())

    def out_half(cc):
        return src.at[pl.ds(pl.multiple_of(8 * cc, 8), 8), :]

    give_near = copy_to(out_half(other), slot(sg, 0, z, other, both), dev(cc=other), k_near, s_near)
    give_far = [copy_to(out_half(cc), slot(sg, 0, z, cc, both), dev(zz=opp, cc=cc), k_far, s_far[cc]) for cc in (0, 1)]
    take_near = copy_to(out_half(0), slot(sg, 0, z, core, both), dev(cc=other), k_near)
    take_far = copy_to(out_half(0), slot(sg, 0, opp, core, both), dev(zz=opp), k_far)

    k_t = [(number(), number()) for _ in range(PARTS)]
    s_t = [(leave(), leave()) for _ in range(PARTS)]
    parts = [pl.ds(k * PART, PART) for k in range(PARTS)]

    def tslot(dy, cc, rows=None, cols=slice(None)):
        start, size = (0, 32) if rows is None else rows
        return tg.at[pl.ds(pl.multiple_of(64 * wrap(y + dy) + 32 * cc + start, 16), size), cols]

    def tcopy(device, k, which):
        return pltpu.make_async_remote_copy(
            src_ref=tgt.at[:, parts[k]], dst_ref=tslot(0, core, cols=parts[k]),
            send_sem=send_sem.at[s_t[k][which]], recv_sem=recv_sem.at[k_t[k][0] + core],
            device_id=device, device_id_type=MESH,
        )

    give_t = [tcopy(dev(zz=opp, cc=1), k, 0) for k in range(PARTS)]
    give_t_here = [tcopy(dev(cc=0), k, 1) for k in range(PARTS)]
    take_t = [
        [copy_to(tgt.at[:, parts[k]], tslot(0, cc, cols=parts[k]), dev(zz=opp, cc=1), k_t[k][cc]) for cc in (0, 1)]
        for k in range(PARTS)
    ]

    def targets_out(k):
        give_t[k].start()

        @pl.when(core == 1)
        def _():
            give_t_here[k].start()

    targets_out(0)

    @pl.when(mine)
    def _():
        give_near.start()

    @pl.when(jnp.logical_not(mine))
    def _():
        give_far[0].start()
        give_far[1].start()

    for k in range(1, PARTS):
        targets_out(k)
    small = [
        send(own.at[0], far.at[0], dev(cc=other)),
        send(own.at[1], far.at[1], dev(cc=other)),
        send(own.at[2, :, pl.ds(0, COLS)], far.at[2, :, pl.ds(0, COLS)], dev(zz=opp)),
    ]

    @pl.when(mine)
    def _():
        slot(sg, 0, z, core, both)[...] = out_half(core)[...]

    @pl.when(core == 0)
    def _():
        tslot(0, 0)[...] = tgt[...]

    @pl.when(jnp.logical_not(mine))
    def _():
        take_near.wait_recv()

    gathers = [Gather(sg, n, CHUNK) for n in range(CHUNKS)]
    for g in gathers:
        g.near()

    yc = {}
    s_y = [leave() for _ in range(PARTS)]
    for k in range(PARTS):
        all_left(tg.at[0:192, parts[k]], s_y[k])

    k_f = [number() for _ in range(PARTS)]

    def targets_start(k):
        for cc in (0, 1):
            if cc == 0:

                @pl.when(core == 1)
                def _():
                    take_t[k][0].wait_recv()
            else:
                take_t[k][1].wait_recv()
            ref = tslot(0, cc, cols=parts[k])
            for d in (1, -1):
                yc[k, cc, d] = send(ref, ref, dev(dy=d), s_y[k])

    targets_start(0)
    take_far.wait_recv()
    for g in gathers:
        g.far()
    for g in gathers:
        g.far_x()

    def targets_on(k):
        for cc in (0, 1):
            for d in (1, -1):
                yc[k, cc, d].wait_recv()
                ref = tslot(-d, cc, (0 if d == 1 else 16, 16), parts[k])
                send(ref, ref, dev(dy=d), s_y[k], k_f[k])

    def targets_in(k):
        ref = tg.at[0:64, parts[k]]
        copy_to(ref, ref, dev(dy=1), k_f[k]).wait_recv()
        cols = slice(k * PART, k * PART + PART)
        half_t[:, cols] = 0.5 * jnp.sum(tg[:, cols] * tg[:, cols], axis=0, keepdims=True)
        for b in range(k * PART // 128, (k + 1) * PART // 128):
            here = slice(128 * b, 128 * b + 128)
            high, low = halves(tg[:, here].T * SCALE)
            tcat[here, 0:256] = high
            tcat[here, 256:512] = high
            tcat[here, 512:768] = low
            cb[here, :] = jnp.broadcast_to(half_t[:, here] * SCALE, (128, 128)).T

    gathers[0].near_on()
    for k in range(1, PARTS):
        targets_start(k)
    for g in gathers[1:]:
        g.near_on()
    targets_on(0)
    for g in gathers:
        g.far_mate()
        g.far_on()
    for k in range(1, PARTS):
        targets_on(k)
    gathers[0].last()
    targets_in(0)

    def split_points(buf, n):
        cols = pl.ds(pl.multiple_of(n * WIDTH, WIDTH), WIDTH)
        a = buf[:, cols]
        high, low = halves(a)
        scat[0:256, cols] = high
        scat[256:512, cols] = low
        scat[512:768, cols] = high
        return 0.5 * jnp.sum(a * a, axis=0, keepdims=True)

    def split_chunk(buf, n, size, norm):
        def step(m, _):
            cols = pl.ds(pl.multiple_of(m * WIDTH, WIDTH), WIDTH)
            norm(cols, split_points(buf, m))
            return 0

        lax.fori_loop(n * size // WIDTH, (n + 1) * size // WIDTH, step, 0)

    def blocks(n, size):
        return [slice(k, k + BLOCK) for k in range(n * size, (n + 1) * size, BLOCK)]

    def wide(a, pieces):
        return jnp.concatenate([a] * pieces, axis=1)

    def lane_top(a):
        return functools.reduce(jnp.maximum, [a[:, k : k + 128] for k in range(0, a.shape[1], 128)])

    def row_pass(body, first=0, size=COLS):
        def step(r, acc):
            return acc + body(pl.ds(pl.multiple_of(r * 8, 8), 8))

        acc = lax.fori_loop(first // 8, (first + size) // 8, step, jnp.zeros((8, ROWS), F32), unroll=8)
        return jnp.sum(acc, axis=0, keepdims=True)

    row_lse = []
    for k in range(PARTS):
        here = slice(k * PART, k * PART + PART)
        if k > 0:
            targets_in(k)

        for n, g in enumerate(gathers):
            if k == 0:
                if n > 0:
                    g.last()
                g.finish()

                def norm(cols, value):
                    frow[:, cols] = value

                split_chunk(sg, n, CHUNK, norm)
            for cols in blocks(n, CHUNK):
                cross = jnp.dot(tcat[here, :], scat[:, cols], preferred_element_type=F32)
                q[here, cols] = cross
                phi[:, cols] = jnp.max(cross - wide(cb[here, :], BLOCK // 128), axis=0, keepdims=True)
        top = phi[...]
        row_lse.append(top + jnp.log(row_pass(lambda rows: jnp.exp2(q[rows, :] - wide(cb[rows, :], ROWS // 128) - top), k * PART, PART)) * LOG2E)

    arrived(small)
    slw[...] = jnp.where(mine, own[0], far[0])
    tim[...] = jnp.where(mine, own[1], far[1])
    tlw[...] = jnp.where(core == 0, own[2], far[2])[:, 0:COLS]

    for k in range(PARTS):
        give_t[k].wait_send()

    @pl.when(core == 1)
    def _():
        for k in range(PARTS):
            give_t_here[k].wait_send()

    @pl.when(mine)
    def _():
        give_near.wait_send()

    @pl.when(jnp.logical_not(mine))
    def _():
        give_far[0].wait_send()
        give_far[1].wait_send()

    copies = to_group(vr.at[0], lse_over_first(jnp.stack(row_lse)))
    arrived(copies)
    lse = lse_over_first(vr[0])
    phi[...] = slw[...] * LOG2E - lse
    frow[...] = frow[...] + EPSILON * (slw[...] - LN2 * lse)

    def join_tops():
        for b in range(0, COLS, 128):
            nb[b : b + 128, :] = jnp.broadcast_to(jnp.max(nb[b : b + 128, :], axis=1, keepdims=True), (128, 128))

    def top_step(r, _):
        rows = pl.ds(pl.multiple_of(r * 8, 8), 8)
        nb[rows, :] = lane_top(q[rows, :] + phi[...])
        return 0

    def exp_step(r, _):
        rows = pl.ds(pl.multiple_of(r * 8, 8), 8)
        p = jnp.exp2(q[rows, :] + phi[...] - wide(nb[rows, :], ROWS // 128))
        e[rows, :] = p
        sb[rows, :] = tiles(p)
        return 0

    def column_lse():
        return column_top(nb), column_sum(sb)

    lax.fori_loop(0, COLS // 8, top_step, 0, unroll=8)
    join_tops()
    lax.fori_loop(0, COLS // 8, exp_step, 0, unroll=4)
    ntop, total = column_lse()
    copies = to_line(vc.at[0], ntop + jnp.log(total) * LOG2E)

    def split_step(r, _):
        rows = pl.ds(pl.multiple_of(r * 16, 16), 16)
        high, low = halves(e[rows, :])
        eh[rows, :] = high
        el[rows, :] = low
        return 0

    lax.fori_loop(0, COLS // 16, split_step, 0, unroll=2)
    arrived(copies)
    factor = jnp.exp2(ntop + (tlw[...] * LOG2E - lse_over_first(vc[0])))
    as_column(factor, cb)

    def against_column(rows):
        return e[rows, :] * wide(cb[rows, :], ROWS // 128)

    copies = to_group(vr.at[1], row_pass(against_column))
    arrived(copies)
    total = jnp.sum(vr[1], axis=0)
    f2[...] = frow[...] + EPSILON * (slw[...] - jnp.log(total))
    phi[...] = jnp.exp(slw[...]) / total
    potential = send(f2, ff, dev(zz=opp))

    def weigh_step(r, _):
        rows = pl.ds(pl.multiple_of(r * 8, 8), 8)
        sb[rows, :] = tiles(e[rows, :] * phi[...])
        return 0

    lax.fori_loop(0, COLS // 8, weigh_step, 0, unroll=8)
    copies = to_line(vc.at[1], factor * column_sum(sb))
    arrived(copies)
    dual = factor * (jnp.exp(tlw[...]) / jnp.sum(vc[1], axis=0))

    potential.wait_recv()

    high, low = halves(tg[...] * dual)
    tw[0:256, :] = high
    tw[256:512, :] = low
    def wz(zz, cols, dx=None):
        return w.at[slice(None) if dx is None else wrap(x + dx), zz, core, :, cols]

    c = {}

    s_w = [leave() for _ in range(PIECES)]
    for n in range(PIECES):
        all_left(mg.at[0:240, chunk_cols(n)], s_w[n])

    def weigh(m):
        cols = slice(m * PIECE, m * PIECE + PIECE)
        acc = jnp.dot(tw[0:256, :], eh[:, cols], preferred_element_type=F32)
        acc = acc + jnp.dot(tw[0:256, :], el[:, cols], preferred_element_type=F32)
        acc = acc + jnp.dot(tw[256:512, :], eh[:, cols], preferred_element_type=F32)
        w[:, :, :, :, cols] = acc.reshape(SIDE, SIDE, 2, 8, PIECE)
        c[m, "core"] = send(w.at[:, :, other, :, cols], r0.at[:, :, :, cols], dev(cc=other), s_w[m])

    def rx_start(n, key, zz, k):
        for d in (1, -1):
            cut = chunk_half(n, d)
            c[n, key, d] = send(wz(zz, cut, 2), rx1.at[k, :, cut], dev(d), s_w[n])

    def rx_middle(n, key, zz, k):
        for d in (1, -1):
            cut = chunk_half(n, d)
            c[n, key, d].wait_recv()
            ref = wz(zz, cut, d)
            ref[...] = ref[...] + rx1[k, :, cut]
            c[n, key, "s", d] = send(wz(zz, chunk_cols(n), d), rx2.at[k, 0 if d == 1 else 1, :, chunk_cols(n)], dev(d), s_w[n])

    def rx_end(n, key, zz, k):
        for d in (1, -1):
            c[n, key, "s", d].wait_recv()
        cols = chunk_cols(n)
        return wz(zz, cols, 0)[...] + rx2[k, 0, :, cols] + rx2[k, 1, :, cols]

    def rx_direct(n, key, zz, k):
        c[n, key] = number()
        for i, d in enumerate((2, 1, -1)):
            send(wz(zz, chunk_cols(n), d), rd.at[k, i, :, chunk_cols(n)], dev(d), s_w[n], c[n, key])

    def rx_sum(n, key, zz, k):
        cols = chunk_cols(n)
        ref = rd.at[k, :, :, cols]
        copy_to(ref, ref, dev(1), c[n, key]).wait_recv()
        return wz(zz, cols, 0)[...] + rd[k, 0, :, cols] + rd[k, 1, :, cols] + rd[k, 2, :, cols]

    def rs1(n):
        cols = chunk_cols(n)
        c[n, "core"].wait_recv()
        ref = w.at[:, :, core, :, cols]
        ref[...] = ref[...] + r0[:, :, :, cols]
        c[n, "mate"] = send(wz(mate, cols), rb.at[:, :, cols], dev(zz=mate), s_w[n])
        rx_direct(n, "m", mates_opp, 0)
        rx_start(n, "o", opp, 0)

    def rs2(n):
        cols = chunk_cols(n)
        c[n, "mate"].wait_recv()
        ref = wz(z, cols)
        ref[...] = ref[...] + rb[:, :, cols]
        rx_direct(n, "z", z, 1)
        rx_middle(n, "o", opp, 0)

    def rs3(n):
        cols = chunk_cols(n)
        qs = wz(mates_opp, cols, 0)
        qs[...] = rx_sum(n, "m", mates_opp, 0)
        c[n, "last"] = send(qs, qb.at[:, cols], dev(zz=mate), s_w[n])

    def point_rows(zz):
        return pl.ds(pl.multiple_of((x * SIDE + zz) * 16 + 8 * core, 8), 8)

    mgathers = [Gather(mg, n, PIECE) for n in range(PIECES)]
    k_out = [(number(), number()) for _ in range(PIECES)]
    s_out = [(leave(), leave()) for _ in range(PIECES)]
    outs = []

    def rs4(n):
        cols = chunk_cols(n)
        g = mgathers[n]
        ratio = tim[:, cols] / jnp.sum(vr[2, :, :, cols], axis=0)
        keep = 1.0 - tim[:, cols]
        share = rx_sum(n, "z", z, 1)
        mg[point_rows(z), cols] = keep * sg[point_rows(z), cols] + ratio * share
        g.near()
        share = rx_end(n, "o", opp, 0)
        c[n, "last"].wait_recv()
        mg[point_rows(opp), cols] = keep * sg[point_rows(opp), cols] + ratio * (share + qb[:, cols])
        g.far()
        g.far_x()
        here = mv.at[pl.ds(pl.multiple_of(8 * core, 8), 8), cols]
        there = mv.at[pl.ds(pl.multiple_of(8 * other, 8), 8), cols]

        def result(zz, device, k):
            return pltpu.make_async_remote_copy(
                src_ref=slot(mg, 0, zz, core, cols), dst_ref=here, send_sem=send_sem.at[k], recv_sem=recv_sem.at[k_out[n][0] + core],
                device_id=device, device_id_type=MESH,
            )

        far_out = result(opp, dev(zz=opp, cc=block), s_out[n][0])
        near_out = result(z, dev(cc=other), s_out[n][1])
        far_out.start()
        started.append(far_out)

        @pl.when(mine)
        def _():
            here[...] = mg[point_rows(z), cols]

        @pl.when(jnp.logical_not(mine))
        def _():
            near_out.start()

        def result_in(ref, k):
            return pltpu.make_async_remote_copy(
                src_ref=ref, dst_ref=ref, send_sem=send_sem.at[s_out[n][0]], recv_sem=recv_sem.at[k],
                device_id=dev(cc=other), device_id_type=MESH,
            )

        outs.append((near_out, result_in(here, k_out[n][0] + core), result_in(there, k_out[n][0] + other)))

    def gather_on(n):
        mgathers[n].near_on()
        mgathers[n].far_mate()
        mgathers[n].far_on()

    weigh(0)
    weigh(1)
    rs1(0)
    as_column(dual, cb)
    copies = to_group(vr.at[2], row_pass(against_column))
    weigh(2)
    rs1(1)
    weigh(3)
    rs2(0)
    rs3(0)
    rs1(2)
    rs2(1)
    rs3(1)
    rs1(3)
    arrived(copies)
    rs4(0)
    rs2(2)
    rs3(2)
    rs4(1)
    gather_on(0)
    rs2(3)
    rs3(3)
    rs4(2)
    gather_on(1)
    rs4(3)
    mgathers[0].last()
    gather_on(2)

    def last_chunk(n):
        def norm(cols, value):
            phi[:, cols] = (f2[:, cols] - value) * SCALE

        split_chunk(mg, n, PIECE, norm)
        cols = slice(n * PIECE, n * PIECE + PIECE)
        scores = jnp.dot(tcat[...], scat[:, cols], preferred_element_type=F32) + phi[:, cols]
        q[:, cols] = scores
        if n == 0:
            nb[...] = lane_top(scores)
        else:
            fresh = jnp.maximum(nb[...], lane_top(scores))
            sb[...] = sb[...] * jnp.exp2(nb[...] - fresh)
            nb[...] = fresh

        def step(r, _):
            rows = pl.ds(pl.multiple_of(r * 8, 8), 8)
            part_sum = tiles(jnp.exp2(q[rows, cols] - wide(nb[rows, :], PIECE // 128)))
            sb[rows, :] = part_sum if n == 0 else sb[rows, :] + part_sum
            return 0

        lax.fori_loop(0, COLS // 8, step, 0, unroll=8)

    def last_lse():
        cb[...] = nb[...]
        join_tops()
        sb[...] = sb[...] * jnp.exp2(cb[...] - nb[...])
        ntop, total = column_lse()
        return ntop + jnp.log(total) * LOG2E

    def results():
        for near_out, half_here, half_there in outs:
            half_there.wait_recv()

            @pl.when(jnp.logical_not(mine))
            def _():
                half_here.wait_recv()
                near_out.wait_send()

        fr[...] = jnp.where(mine, f2[...], ff[...])
        for store in stores[:2]:
            store.start()

    mgathers[0].finish()
    last_chunk(0)
    results()
    mgathers[1].last()
    gather_on(3)
    mgathers[1].finish()
    last_chunk(1)
    mgathers[2].last()
    mgathers[2].finish()
    last_chunk(2)
    mgathers[3].last()
    mgathers[3].finish()
    last_chunk(3)

    home = z + core * (opp - z)
    part[...] = last_lse() - half_t[...] * SCALE

    def to_owner(dy, cc, k, base):
        return pltpu.make_async_remote_copy(
            src_ref=part, dst_ref=vc.at[2, line_slot], send_sem=send_sem.at[k], recv_sem=recv_sem.at[base + core],
            device_id=dev(dy=dy, zz=home, cc=cc), device_id_type=MESH,
        )

    def from_owner(k):
        return copy_to(part, vc.at[2, line_slot], dev(cc=other), k)

    waits = []
    for dy in (2, 1, -1):
        base, more = number(), number()
        for cc in (0, 1):
            copy = to_owner(dy, cc, leave(), base)
            copy.start()
            started.append(copy)
        waits += [from_owner(base), from_owner(more)]
    base, more = number(), number()
    to_one, to_zero = to_owner(0, 1, leave(), base), to_owner(0, 0, leave(), base)
    to_one.start()
    started.append(to_one)

    @pl.when(core == 1)
    def _():
        to_zero.start()
        from_owner(base).wait_recv()

    @pl.when(core == 0)
    def _():
        vc[2, line_slot] = part[...]

    from_owner(more).wait_recv()
    arrived(waits)
    fc[...] = EPSILON * (own[2][:, 0:COLS] - LN2 * lse_over_first(vc[2]))
    stores[2].start()
    for store in stores:
        store.wait()

    @pl.when(core == 1)
    def _():
        to_zero.wait_send()

    for copy in started:
        copy.wait_send()


def per_device(sources, targets, source_logw, target_logw, times):
    anywhere = pl.BlockSpec(memory_space=pl.ANY)
    rowp, moved, colp = pl.pallas_call(
        kernel,
        out_shape=(
            jax.ShapeDtypeStruct((1, ROWS), F32),
            jax.ShapeDtypeStruct((16, ROWS), F32),
            jax.ShapeDtypeStruct((1, COLS), F32),
        ),
        in_specs=[anywhere] * 5,
        out_specs=(anywhere,) * 3,
        scratch_shapes=[
            pltpu.VMEM((16, ROWS), F32),
            pltpu.VMEM((32, COLS), F32),
            pltpu.VMEM((3, 1, ROWS), F32),
            pltpu.VMEM((3, 1, ROWS), F32),
            pltpu.VMEM((1, ROWS), F32),
            pltpu.VMEM((1, COLS), F32),
            pltpu.VMEM((1, ROWS), F32),
            pltpu.VMEM((FEATURES, ROWS), F32),
            pltpu.VMEM((FEATURES, COLS), F32),
            pltpu.VMEM((FEATURES, ROWS), F32),
            pltpu.VMEM((16, ROWS), F32),
            pltpu.VMEM((COLS, 3 * FEATURES), BF16),
            pltpu.VMEM((3 * FEATURES, ROWS), BF16),
            pltpu.VMEM((COLS, ROWS), F32),
            pltpu.VMEM((COLS, ROWS), F32),
            pltpu.VMEM((SIDE, SIDE, 2, 8, ROWS), F32),
            pltpu.VMEM((2 * FEATURES, COLS), BF16),
            pltpu.VMEM((COLS, ROWS), BF16),
            pltpu.VMEM((COLS, ROWS), BF16),
            pltpu.VMEM((SIDE, SIDE, 8, ROWS), F32),
            pltpu.VMEM((SIDE, 8, ROWS), F32),
            pltpu.VMEM((1, 8, ROWS), F32),
            pltpu.VMEM((1, 2, 8, ROWS), F32),
            pltpu.VMEM((2, 3, 8, ROWS), F32),
            pltpu.VMEM((8, ROWS), F32),
            pltpu.VMEM((3, GROUP, 1, ROWS), F32),
            pltpu.VMEM((3, LINE, 1, COLS), F32),
            pltpu.VMEM((COLS, 128), F32),
            pltpu.VMEM((COLS, 128), F32),
            pltpu.VMEM((COLS, 128), F32),
            pltpu.VMEM((1, COLS), F32),
            pltpu.VMEM((1, ROWS), F32),
            pltpu.VMEM((1, ROWS), F32),
            pltpu.VMEM((1, ROWS), F32),
            pltpu.VMEM((1, ROWS), F32),
            pltpu.VMEM((1, ROWS), F32),
            pltpu.VMEM((1, COLS), F32),
            pltpu.VMEM((1, COLS), F32),
            pltpu.SemaphoreType.DMA((DEPARTURES,)),
            pltpu.SemaphoreType.DMA((ARRIVALS,)),
            pltpu.SemaphoreType.DMA((5,)),
        ],
        compiler_params=pltpu.CompilerParams(
            collective_id=0, has_side_effects=True, vmem_limit_bytes=60 * 1024 * 1024
        ),
    )(sources, targets, source_logw[None], target_logw[None], times[None])
    return rowp[0], moved, colp[0]


def solution(mesh):
    return jax.shard_map(
        per_device,
        mesh=mesh,
        in_specs=(P("tgt", "src"), P("src", "tgt"), P("src"), P("tgt"), P("src")),
        out_specs=(P("src"), P("tgt", "src"), P("tgt")),
        check_vma=False,
    )
```
